32 devices in a mesh: groups: 2 (over x), wide: 8 (over z, y), ffn: 2 (over core).
Axes of the slice: x: 2, y: 2, z: 4, core: 2. Of those that a mesh axis runs over, the one named last changes fastest.
Arguments:
- tokens: bfloat16 [64, 8192], P('groups', 'wide'), parts along dimension 0, may hold values from -25 to 25
- gate_weight: bfloat16 [8192, 26624], P('wide', 'ffn'), may hold values from -0.09375 to 0.09375
- up_weight: bfloat16 [8192, 26624], P('wide', 'ffn'), may hold values from -0.09375 to 0.09375
- down_weight: bfloat16 [26624, 8192], P('ffn', 'wide'), may hold values from -0.0390625 to 0.0390625
Outputs:
- state: float32 [64, 8192], P('groups', 'wide'), parts along dimension 0
The draws below stay inside these ranges and needn't reach their ends.
There are 2 independent parts, one for each index of `groups`. The reference program is written for one: setup_inputs(seed, part) draws one part's arguments, and reference() takes and returns one part's arrays. A program takes and returns all parts, laid end to end along the dimension named above; an argument that names none is the same for every part. Nothing has to cross between parts.
All inputs are finite; a program needn't handle non-finite values.
Results may differ from the reference program's by a relative error of at most 0.0053.
Values may be sent and summed in bfloat16 or wider, within the bound.
No kernel may reach another device: no remote copies, remote signals or barrier semaphores. Data moves between devices by JAX's collectives and lax.ppermute only.
A program may use at most 192 MiB of HBM per device.

```python
import jax
import jax.numpy as jnp
from jax import lax

D = 8192
FF = 26624
ROWS = 32
STEPS = 2


def draw_tokens(key, part):
    key = jax.random.fold_in(key, 11)
    key_col, key_row, key_base = jax.random.split(key, 3)
    position = jnp.arange(D, dtype=jnp.float32) / D
    col_scale = jnp.power(10.0, jax.random.uniform(key_col, (D,), jnp.float32, -0.5, 0.5)) * jnp.sqrt(0.5 + 1.5 * position)
    row_scale = jnp.power(10.0, jax.random.uniform(key_row, (ROWS, 1), jnp.float32, -0.5, 0.5))
    base = jnp.clip(jax.random.normal(key_base, (ROWS, D), jnp.float32), -5.0, 5.0)
    return (0.3 * row_scale * col_scale * base).astype(jnp.bfloat16)


def raised(result, key, source, target, shards_of, factor):
    owner, partner = [(jnp.arange(result.shape[dim]) // (result.shape[dim] // shards_of)).reshape([-1 if axis == dim else 1 for axis in range(result.ndim)]) for dim in (source, target)]
    chosen = jax.random.permutation(key, shards_of)[partner]
    strong = (owner == chosen) | (owner == (partner + shards_of // 2) % shards_of)
    return jnp.where(strong, factor * result, result)


def shard_levels(key, extent, shards, least, top_value):
    def one(axis_at, shards_of):
        heights = jax.random.uniform(jax.random.fold_in(jax.random.fold_in(key, 6), axis_at), (shards_of,), jnp.float32, least / len(shards), top_value / len(shards))
        return jnp.repeat(jnp.exp(heights), extent[axis_at] // shards_of).reshape((-1,) + (1,) * (len(extent) - axis_at - 1))

    factor_of = one(*shards[0])
    for cut in shards[1:]:
        factor_of = factor_of * one(*cut)
    return factor_of


def gaussian(rng, dims, spread, limit, pieces=(), held_as=jnp.bfloat16):
    array = jax.random.normal(rng, dims, jnp.float32) * spread
    if len(pieces) > 0:
        array = shard_levels(rng, dims, pieces, -0.22, 0.18) * array
    return jnp.clip(array, min=-limit, max=limit).astype(held_as)


def bell_draw_with(stream_key, dims, deviation, reach, pieces, heavy, kind=jnp.bfloat16):
    drawn = deviation * jax.random.normal(stream_key, dims, jnp.float32)
    if pieces:
        drawn = drawn * shard_levels(stream_key, dims, pieces, -0.22, 0.18)
    return jnp.clip(raised(drawn, jax.random.fold_in(stream_key, 3), *heavy), -reach, reach).astype(kind)


def setup_inputs(seed: int = 0, part: int = 0) -> dict:
    splits = jax.random.split(jax.random.key(seed), 5)
    own_keys = jax.random.split(jax.random.fold_in(splits[4], part), 5)
    return {
        "tokens": draw_tokens(jax.random.fold_in(jax.random.fold_in(splits[4], part), 71), part),
        "gate_weight": bell_draw_with(splits[1], (D, FF), D ** -0.5, 0.09375, ((0, 8), (1, 2)), (0, 1, 8, 2.0)),
        "up_weight": bell_draw_with(splits[2], (D, FF), D ** -0.5, 0.09375, ((0, 8), (1, 2)), (0, 1, 8, 2.0)),
        "down_weight": gaussian(splits[3], (FF, D), FF ** -0.5, 0.0390625, ((0, 2), (1, 8))),
    }


def reference(tokens, gate_weight, up_weight, down_weight):
    state = tokens.astype(jnp.float32)
    for step in range(STEPS):
        meansq = lax.optimization_barrier(jnp.mean(state * state, axis=1, keepdims=True))
        normed = (state / jnp.sqrt(meansq + 1e-05)).astype(jnp.bfloat16)
        gate = jnp.dot(normed, gate_weight, preferred_element_type=jnp.float32)
        up = jnp.dot(normed, up_weight, preferred_element_type=jnp.float32)
        hidden = (jax.nn.silu(gate) * up).astype(jnp.bfloat16)
        change = jnp.dot(hidden, down_weight, preferred_element_type=jnp.float32)
        state = state + change
    return state
```

```python
import functools

import jax
import jax.numpy as jnp
from jax import lax
from jax.experimental import pallas as pl
from jax.experimental.pallas import tpu as pltpu
from jax.sharding import PartitionSpec as P

STEPS = 2
CHUNKS = 2
LANES = 128
PIECE = 256
F32 = jnp.float32
BF16 = jnp.bfloat16
SMEM = pl.BlockSpec(memory_space=pltpu.SMEM)
VMEM = pl.BlockSpec(memory_space=pltpu.VMEM)
HBM = pl.BlockSpec(memory_space=pltpu.HBM)
MIB = 2**20


def struct(shape, dtype):
    return jax.ShapeDtypeStruct(shape, dtype)


def cost(flops, moved):
    return pl.CostEstimate(flops=int(flops), bytes_accessed=int(moved), transcendentals=0)


def stages_of(wide):
    found, low = [], 0
    while (1 << low) < wide:
        bits = 1 if low == 0 else min(2, wide.bit_length() - 1 - low)
        found.append((low, 1 << bits))
        low += bits
    return found


def offsets_of(stages):
    found = [0]
    for low, size in reversed(stages):
        found = [(i << low) ^ rest for i in range(size) for rest in found]
    return found


def swap(value, axis, flip, count):
    return lax.ppermute(value, axis, [(i, i ^ flip) for i in range(count)])


def cuts_of(extent, piece):
    return [(a, min(a + piece, extent)) for a in range(0, extent, piece)]


def rows_mean_square(rows):
    total = jnp.sum(rows * rows, axis=1, keepdims=True)
    return jnp.broadcast_to(total, (rows.shape[0], LANES))


def arrange_kernel(offsets, per, groups, where_ref, own_ref, *refs):
    others, (state_ref, x_ref, sumsq_ref, whole) = refs[: groups - 1], refs[groups - 1 :]
    me, group = where_ref[0], where_ref[1]
    rows = own_ref.shape[0]
    for k, ref in enumerate((own_ref,) + tuple(others)):
        start = lax.rem(group + k, groups) * rows
        whole[pl.ds(pl.multiple_of(start, 8), rows), :] = ref[...].astype(F32)
    for p, offset in enumerate(offsets):
        first = (me ^ offset) * per
        if per % 8 == 0:
            first = pl.multiple_of(first, 8)
        state_ref[p * per : (p + 1) * per, :] = whole[pl.ds(first, per), :]
    state = state_ref[...]
    x_ref[...] = state.astype(BF16)
    sumsq_ref[...] = rows_mean_square(state)


def arrange(offsets, per, groups, where, own, others):
    rows, width = own.shape
    rows *= groups
    return pl.pallas_call(
        functools.partial(arrange_kernel, offsets, per, groups),
        out_shape=(struct((rows, width), F32), struct((rows, width), BF16), struct((rows, LANES), F32)),
        in_specs=[SMEM] + [VMEM] * groups,
        out_specs=(VMEM,) * 3,
        scratch_shapes=[pltpu.VMEM((rows, width), F32)],
        name="arrange",
        cost_estimate=cost(rows * width, rows * width * 10),
    )(where, own, *others)


def gate_up_kernel(first, per, base_ref, x_ref, gate_hbm, up_hbm, keep_ref, *refs):
    sends, (gate_vmem, up_vmem, sems) = refs[:-3], refs[-3:]
    depth, width = gate_vmem.shape
    column = pl.multiple_of(base_ref[0] + first, LANES)
    cuts = cuts_of(depth, PIECE)
    copies = []
    for i, (a, b) in enumerate(cuts):
        for k, (source, target) in enumerate(((gate_hbm, gate_vmem), (up_hbm, up_vmem))):
            copy = pltpu.make_async_copy(
                source.at[pl.ds(a, b - a), pl.ds(column, width)], target.at[pl.ds(a, b - a), :], sems.at[k, i]
            )
            copy.start()
            copies.append(copy)
    totals = [None, None]
    for i, (a, b) in enumerate(cuts):
        piece = x_ref[:, a:b]
        for k, held in enumerate((gate_vmem, up_vmem)):
            copies[2 * i + k].wait()
            term = jnp.dot(piece, held[a:b, :], preferred_element_type=F32)
            totals[k] = term if totals[k] is None else totals[k] + term
    group = keep_ref.shape[0]
    for p in range(group * (1 + len(sends))):
        rows = slice(p * per, (p + 1) * per)
        both = jnp.concatenate([totals[0][rows], totals[1][rows]], axis=0)
        target = ((keep_ref,) + tuple(sends))[p // group]
        target[p % group] = both.astype(target.dtype)


def gate_up(first, width, per, size, base, x, gate_weight, up_weight):
    rows, depth = x.shape
    group = rows // per // size
    shape = (group, 2 * per, width)
    return pl.pallas_call(
        functools.partial(gate_up_kernel, first, per),
        out_shape=(struct(shape, F32),) + (struct(shape, BF16),) * (size - 1),
        in_specs=[SMEM, VMEM, HBM, HBM],
        out_specs=(VMEM,) * size,
        scratch_shapes=[
            pltpu.VMEM((depth, width), BF16),
            pltpu.VMEM((depth, width), BF16),
            pltpu.SemaphoreType.DMA((2, len(cuts_of(depth, PIECE)))),
        ],
        name="gate_up",
        compiler_params=pltpu.CompilerParams(vmem_limit_bytes=44 * MIB),
        cost_estimate=cost(4 * rows * depth * width, 4 * depth * width),
    )(base, x, gate_weight, up_weight)


def add_kernel(count, keep_ref, *refs):
    arrived, outs = refs[:count], refs[count:]
    total = keep_ref[...]
    for ref in arrived:
        total = total + ref[...].astype(F32)
    group = outs[0].shape[0]
    for i, out in enumerate(outs):
        out[...] = total[i * group : (i + 1) * group].astype(out.dtype)


def add_stage(keep, arrived, size):
    shape = (keep.shape[0] // size,) + keep.shape[1:]
    return pl.pallas_call(
        functools.partial(add_kernel, len(arrived)),
        out_shape=(struct(shape, F32),) + (struct(shape, BF16),) * (size - 1),
        in_specs=[VMEM] * (1 + len(arrived)),
        out_specs=(VMEM,) * size,
        name="add_partials",
        compiler_params=pltpu.CompilerParams(vmem_limit_bytes=8 * MIB),
        cost_estimate=cost(keep.size * 2, keep.size * 10),
    )(keep, *arrived)


def hidden_kernel(count, width, keep_ref, *refs):
    arrived, (sumsq_ref, out_ref) = refs[:count], refs[count:]
    total = keep_ref[0]
    for ref in arrived:
        total = total + ref[0].astype(F32)
    per = out_ref.shape[0]
    scale = 1.0 / jnp.sqrt(sumsq_ref[...][:, :1] / width + 1e-05)
    gate, up = total[:per] * scale, total[per:] * scale
    out_ref[...] = (gate / (1.0 + jnp.exp(-gate)) * up).astype(BF16)


def hidden_of(keep, arrived, sumsq, features):
    _, both, width = keep.shape
    return pl.pallas_call(
        functools.partial(hidden_kernel, len(arrived), features),
        out_shape=struct((both // 2, width), BF16),
        in_specs=[VMEM] * (2 + len(arrived)),
        out_specs=VMEM,
        name="hidden",
        compiler_params=pltpu.CompilerParams(vmem_limit_bytes=8 * MIB),
        cost_estimate=cost(keep.size * 10, keep.size * 10),
    )(keep, *arrived, sumsq)


def join_kernel(*refs):
    sources, out_ref = refs[:-1], refs[-1]
    out_ref[...] = jnp.concatenate([ref[...].astype(F32) for ref in sources], axis=0).astype(BF16)


def join(parts):
    rows, width = parts[0].shape
    return pl.pallas_call(
        join_kernel,
        out_shape=struct((rows * len(parts), width), BF16),
        in_specs=[VMEM] * len(parts),
        out_specs=VMEM,
        name="join",
        compiler_params=pltpu.CompilerParams(vmem_limit_bytes=8 * MIB),
        cost_estimate=cost(0, rows * len(parts) * width * 4),
    )(*parts)


def down_kernel(first, count, added, base_ref, *refs):
    parts = refs[:count]
    down_hbm = refs[count]
    before = refs[count + 1] if added else None
    out_ref, down_vmem, sems = refs[-3:]
    depth = down_vmem.shape[0]
    row = pl.multiple_of(base_ref[0] + first, LANES)
    cuts = cuts_of(depth, 2 * PIECE)
    copies = []
    for i, (a, b) in enumerate(cuts):
        copy = pltpu.make_async_copy(
            down_hbm.at[pl.ds(row + a, b - a), :], down_vmem.at[pl.ds(a, b - a), :], sems.at[i]
        )
        copy.start()
        copies.append(copy)
    hidden = jnp.concatenate([ref[...] for ref in parts], axis=0)
    total = before[...] if added else None
    for i, (a, b) in enumerate(cuts):
        copies[i].wait()
        term = jnp.dot(hidden[:, a:b], down_vmem[a:b, :], preferred_element_type=F32)
        total = term if total is None else total + term
    out_ref[...] = total


def down(first, base, parts, down_weight, before):
    rows, width = sum(part.shape[0] for part in parts), down_weight.shape[1]
    depth = parts[0].shape[1]
    added = before is not None
    return pl.pallas_call(
        functools.partial(down_kernel, first, len(parts), added),
        out_shape=struct((rows, width), F32),
        in_specs=[SMEM] + [VMEM] * len(parts) + [HBM] + [VMEM] * added,
        out_specs=VMEM,
        scratch_shapes=[
            pltpu.VMEM((depth, width), BF16),
            pltpu.SemaphoreType.DMA((len(cuts_of(depth, 2 * PIECE)),)),
        ],
        name="down",
        compiler_params=pltpu.CompilerParams(vmem_limit_bytes=44 * MIB),
        cost_estimate=cost(2 * rows * depth * width, 2 * depth * width),
    )(base, *parts, down_weight, *([before] if added else []))


def chip_kernel(a_ref, b_ref, state_ref, state_out, send_ref):
    total = a_ref[...] + b_ref[...]
    send_ref[...] = total.astype(BF16)
    state_out[...] = state_ref[...] + total


def renew_kernel(state_ref, *refs):
    arrived, (state_out, x_ref, sumsq_ref) = refs[:-3], refs[-3:]
    state = state_ref[...]
    for ref in arrived:
        state = state + ref[...].astype(F32)
    state_out[...] = state
    x_ref[...] = state.astype(BF16)
    sumsq_ref[...] = rows_mean_square(state)


def finish_kernel(offsets, per, groups, where_ref, a_ref, b_ref, state_ref, out_ref, *refs):
    sends, (change, state) = refs[: groups - 1], refs[groups - 1 :]
    me, group = where_ref[0], where_ref[1]
    for p, offset in enumerate(offsets):
        first = (me ^ offset) * per
        if per % 8 == 0:
            first = pl.multiple_of(first, 8)
        rows = slice(p * per, (p + 1) * per)
        change[pl.ds(first, per), :] = a_ref[rows, :] + b_ref[rows, :]
        state[pl.ds(first, per), :] = state_ref[rows, :]
    rows = out_ref.shape[0]
    own = pl.ds(pl.multiple_of(group * rows, 8), rows)
    out_ref[...] = state[own, :] + change[own, :]
    for k, ref in enumerate(sends):
        other = pl.multiple_of(lax.rem(group + k + 1, groups) * rows, 8)
        ref[...] = change[pl.ds(other, rows), :].astype(BF16)


def per_device(counts, tokens, gate_weight, up_weight, down_weight):
    groups, wide, ffn = counts
    stages = stages_of(wide)
    offsets = offsets_of(stages)
    rows = tokens.shape[0] * groups
    per = rows // wide
    features = tokens.shape[1] * wide
    share = gate_weight.shape[1] // groups
    edges = [share // LANES * k // CHUNKS * LANES for k in range(CHUNKS + 1)]
    chunks = [(a, b - a) for a, b in zip(edges, edges[1:])]
    me, group = lax.axis_index("wide"), lax.axis_index("groups")
    where = jnp.stack([me, group]).astype(jnp.int32)
    base = (group * share).astype(jnp.int32).reshape(1)

    def from_group(value, k):
        return lax.ppermute(value, "groups", [((i + k) % groups, i) for i in range(groups)])

    others = [from_group(tokens, k) for k in range(1, groups)]
    state, x, sumsq = arrange(offsets, per, groups, where, tokens, others)

    def scatter_stage(low, size, sends):
        return [swap(send, "wide", i << low, wide) for i, send in zip(range(1, size), sends)]

    for step in range(STEPS):
        for low, size in stages:
            group_rows = sumsq.shape[0] // size
            blocks = [sumsq[i * group_rows : (i + 1) * group_rows] for i in range(size)]
            sumsq = blocks[0] + sum(scatter_stage(low, size, blocks[1:]))
        change = None
        for first, width in chunks:
            low, size = stages[0]
            keep, *sends = gate_up(first, width, per, size, base, x, gate_weight, up_weight)
            arrived = scatter_stage(low, size, sends)
            for low, size in stages[1:]:
                keep, *sends = add_stage(keep, arrived, size)
                arrived = scatter_stage(low, size, sends)
            parts = [hidden_of(keep, arrived, sumsq, features)]
            for low, size in reversed(stages):
                whole = parts[0] if len(parts) == 1 else join(parts)
                parts = [whole] + [swap(whole, "wide", i << low, wide) for i in range(1, size)]
            change = down(first, base, parts, down_weight, change)
        other = swap(change, "ffn", 1, ffn)
        if step + 1 < STEPS:
            shape = state.shape
            state, send = pl.pallas_call(
                chip_kernel,
                out_shape=(struct(shape, F32), struct(shape, BF16)),
                in_specs=[VMEM] * 3,
                out_specs=(VMEM,) * 2,
                name="chip_sum",
                cost_estimate=cost(state.size, state.size * 16),
            )(change, other, state)
            arrived = [from_group(send, k) for k in range(1, groups)]
            state, x, sumsq = pl.pallas_call(
                renew_kernel,
                out_shape=(struct(shape, F32), struct(shape, BF16), struct((rows, LANES), F32)),
                in_specs=[VMEM] * (1 + len(arrived)),
                out_specs=(VMEM,) * 3,
                name="renew",
                cost_estimate=cost(state.size, state.size * 12),
            )(state, *arrived)
    own = struct(tokens.shape, F32)
    out, *sends = pl.pallas_call(
        functools.partial(finish_kernel, offsets, per, groups),
        out_shape=(own,) + (struct(tokens.shape, BF16),) * (groups - 1),
        in_specs=[SMEM] + [VMEM] * 3,
        out_specs=(VMEM,) * groups,
        scratch_shapes=[pltpu.VMEM(state.shape, F32)] * 2,
        name="finish",
        cost_estimate=cost(state.size, state.size * 16),
    )(where, change, other, state)
    for k, send in enumerate(sends):
        arrived = from_group(send, groups - 1 - k)
        out = out + arrived.astype(F32)
    return out


def solution(mesh):
    counts = tuple(mesh.shape[axis] for axis in ("groups", "wide", "ffn"))
    return jax.shard_map(
        functools.partial(per_device, counts),
        mesh=mesh,
        in_specs=(P("groups", "wide"), P("wide", "ffn"), P("wide", "ffn"), P("ffn", "wide")),
        out_specs=P("groups", "wide"),
        check_vma=False,
    )
```

```python
import functools

import jax
import jax.numpy as jnp
from jax import lax
from jax.experimental import pallas as pl
from jax.experimental.pallas import tpu as pltpu
from jax.sharding import PartitionSpec as P

STEPS = 2
CHUNKS = 2
LANES = 128
PIECE = 256
F32 = jnp.float32
BF16 = jnp.bfloat16
SMEM = pl.BlockSpec(memory_space=pltpu.SMEM)
VMEM = pl.BlockSpec(memory_space=pltpu.VMEM)
HBM = pl.BlockSpec(memory_space=pltpu.HBM)
MIB = 2**20
LOAD_LIMIT, FRESH_LIMIT, DOWN_LIMIT, HELD_LIMIT = 10, 10, 10, 10


def struct(shape, dtype):
    return jax.ShapeDtypeStruct(shape, dtype)


def in_hbm(value):
    return pltpu.with_memory_space_constraint(value, pltpu.HBM)


def cost(flops, moved):
    return pl.CostEstimate(flops=int(flops), bytes_accessed=int(moved), transcendentals=0)


def stages_of(wide):
    found, low = [], 0
    while (1 << low) < wide:
        bits = 1 if low == 0 else min(2, wide.bit_length() - 1 - low)
        found.append((low, 1 << bits))
        low += bits
    return found


def offsets_of(stages):
    found = [0]
    for low, size in reversed(stages):
        found = [(i << low) ^ rest for i in range(size) for rest in found]
    return found


def swap(value, axis, flip, count):
    return lax.ppermute(value, axis, [(i, i ^ flip) for i in range(count)])


def cuts_of(extent, piece):
    return [(a, min(a + piece, extent)) for a in range(0, extent, piece)]


def rows_mean_square(rows):
    total = jnp.sum(rows * rows, axis=1, keepdims=True)
    return jnp.broadcast_to(total, (rows.shape[0], LANES))


def arrange_kernel(offsets, per, groups, where_ref, own_ref, *refs):
    others, (state_ref, x_ref, sumsq_ref, whole) = refs[: groups - 1], refs[groups - 1 :]
    me, group = where_ref[0], where_ref[1]
    rows = own_ref.shape[0]
    for k, ref in enumerate((own_ref,) + tuple(others)):
        start = lax.rem(group + k, groups) * rows
        whole[pl.ds(pl.multiple_of(start, 8), rows), :] = ref[...].astype(F32)
    for p, offset in enumerate(offsets):
        first = (me ^ offset) * per
        if per % 8 == 0:
            first = pl.multiple_of(first, 8)
        state_ref[p * per : (p + 1) * per, :] = whole[pl.ds(first, per), :]
    state = state_ref[...]
    x_ref[...] = state.astype(BF16)
    sumsq_ref[...] = rows_mean_square(state)


def arrange(offsets, per, groups, where, own, others):
    rows, width = own.shape
    rows *= groups
    return pl.pallas_call(
        functools.partial(arrange_kernel, offsets, per, groups),
        out_shape=(struct((rows, width), F32), struct((rows, width), BF16), struct((rows, LANES), F32)),
        in_specs=[SMEM] + [VMEM] * groups,
        out_specs=(VMEM,) * 3,
        scratch_shapes=[pltpu.VMEM((rows, width), F32)],
        name="arrange",
        compiler_params=pltpu.CompilerParams(vmem_limit_bytes=8 * MIB),
        cost_estimate=cost(rows * width, rows * width * 10),
    )(where, own, *others)


def squeeze(value):
    return (value * jnp.abs(value)).astype(BF16)


def expand(ref, index=slice(None)):
    sent = ref[index].astype(F32)
    return sent * lax.rsqrt(jnp.maximum(jnp.abs(sent), 1e-37))


def three_lanes(value):
    shape = value.shape[:-1] + (LANES,)
    value = jnp.broadcast_to(value, shape)
    lane = lax.broadcasted_iota(jnp.int32, shape, len(shape) - 1)
    out = jnp.zeros(shape, F32)
    for k in range(3):
        part = value.astype(BF16).astype(F32)
        out = jnp.where(lane == k, part, out)
        value = value - part
    return out.astype(BF16)


def start_copies(pairs, sems):
    copies = [pltpu.make_async_copy(source, target, sems.at[i]) for i, (source, target) in enumerate(pairs)]
    for copy in copies:
        copy.start()
    return copies


def column_pairs(column, width, sources, targets):
    pairs = []
    for a, b in cuts_of(targets[0].shape[0], PIECE):
        for source, target in zip(sources, targets):
            pairs.append((source.at[pl.ds(a, b - a), pl.ds(column, width)], target.at[pl.ds(a, b - a), :]))
    return pairs


def load_kernel(first, base_ref, gate_hbm, up_hbm, gate_ref, up_ref, sems):
    column = pl.multiple_of(base_ref[0] + first, LANES)
    for copy in start_copies(column_pairs(column, gate_ref.shape[1], (gate_hbm, up_hbm), (gate_ref, up_ref)), sems):
        copy.wait()


def load(first, width, base, gate_weight, up_weight):
    depth = gate_weight.shape[0]
    shape = struct((depth, width), BF16)
    return pl.pallas_call(
        functools.partial(load_kernel, first),
        out_shape=(shape,) * 2,
        in_specs=[SMEM, HBM, HBM],
        out_specs=(VMEM,) * 2,
        scratch_shapes=[pltpu.SemaphoreType.DMA((2 * len(cuts_of(depth, PIECE)),))],
        name="load",
        compiler_params=pltpu.CompilerParams(vmem_limit_bytes=LOAD_LIMIT * MIB),
        cost_estimate=cost(0, 4 * depth * width),
    )(base, gate_weight, up_weight)


def gate_up_kernel(first, per, size, fresh, summed, base_ref, x_ref, *refs):
    refs = list(refs)
    sumsq_ref = refs.pop(0) if summed else None
    weights, refs = refs[:2], refs[2:]
    outs, refs = refs[:size], refs[size:]
    copies = None
    if fresh:
        held, sems = refs[:2], refs[2]
        column = pl.multiple_of(base_ref[0] + first, LANES)
        copies = start_copies(column_pairs(column, held[0].shape[1], weights, held), sems)
    else:
        held = weights
    depth, width = held[0].shape
    totals = [None, None]
    for i, (a, b) in enumerate(cuts_of(depth, PIECE)):
        piece = x_ref[:, a:b]
        for k, weight in enumerate(held):
            if fresh:
                copies[2 * i + k].wait()
            term = jnp.dot(piece, weight[a:b, :], preferred_element_type=F32)
            totals[k] = term if totals[k] is None else totals[k] + term
    group = outs[0].shape[0]
    for p in range(group * size):
        rows = slice(p * per, (p + 1) * per)
        both = jnp.concatenate([totals[0][rows], totals[1][rows]], axis=0)
        target = outs[p // group]
        target[p % group, :, :width] = both if p < group else squeeze(both)
        if summed:
            square = sumsq_ref[rows]
            square = jnp.concatenate([square, square], axis=0)
            target[p % group, :, width:] = square if p < group else three_lanes(square[:, :1])


def gate_up(first, width, per, size, base, x, sumsq, weights, fresh):
    rows, depth = x.shape
    group = rows // per // size
    summed = sumsq is not None
    shape = (group, 2 * per, width + LANES * summed)
    held = struct((depth, width), BF16)
    return pl.pallas_call(
        functools.partial(gate_up_kernel, first, per, size, fresh, summed),
        out_shape=(struct(shape, F32),) + (struct(shape, BF16),) * (size - 1) + (held,) * (2 * fresh),
        in_specs=[SMEM, VMEM] + [VMEM] * summed + [HBM if fresh else VMEM] * 2,
        out_specs=(VMEM,) * (size + 2 * fresh),
        scratch_shapes=[pltpu.SemaphoreType.DMA((2 * len(cuts_of(depth, PIECE)),))] * fresh,
        name="gate_up",
        compiler_params=pltpu.CompilerParams(vmem_limit_bytes=(FRESH_LIMIT if fresh else HELD_LIMIT) * MIB),
        cost_estimate=cost(4 * rows * depth * width, 4 * depth * width),
    )(base, x, *([sumsq] if summed else []), *weights)


def arrived_sum(keep, width, refs):
    total = keep[..., :width]
    for ref in refs:
        total = total + expand(ref, (slice(None), slice(None), slice(0, width)))
    if keep.shape[-1] == width:
        return total, None
    square = keep[..., width:]
    for ref in refs:
        square = square + jnp.sum(ref[:, :, width:].astype(F32), axis=-1, keepdims=True)
    return total, square


def add_kernel(count, width, keep_ref, *refs):
    arrived, outs = refs[:count], refs[count:]
    total, square = arrived_sum(keep_ref[...], width, arrived)
    group = outs[0].shape[0]
    for i, out in enumerate(outs):
        rows = slice(i * group, (i + 1) * group)
        out[:, :, :width] = total[rows] if i == 0 else squeeze(total[rows])
        if square is not None:
            out[:, :, width:] = square[rows] if i == 0 else three_lanes(square[rows][..., :1])


def add_stage(keep, width, arrived, size):
    shape = (keep.shape[0] // size,) + keep.shape[1:]
    return pl.pallas_call(
        functools.partial(add_kernel, len(arrived), width),
        out_shape=(struct(shape, F32),) + (struct(shape, BF16),) * (size - 1),
        in_specs=[VMEM] * (1 + len(arrived)),
        out_specs=(VMEM,) * size,
        name="add_partials",
        compiler_params=pltpu.CompilerParams(vmem_limit_bytes=8 * MIB),
        cost_estimate=cost(keep.size * 2, keep.size * 10),
    )(keep, *arrived)


def hidden_kernel(count, width, summed, features, keep_ref, *refs):
    arrived, refs = refs[:count], refs[count:]
    total, square = arrived_sum(keep_ref[...], width, arrived)
    total = total[0]
    out_ref = refs[0] if summed else refs[1]
    per = out_ref.shape[0]
    if summed:
        scale = 1.0 / jnp.sqrt(square[0][:per] / features + 1e-05)
        refs[1][...] = scale
    else:
        scale = refs[0][...]
    scale = scale[:, :1]
    gate, up = total[:per] * scale, total[per:] * scale
    out_ref[...] = (gate / (1.0 + jnp.exp(-gate)) * up).astype(BF16)


def hidden_of(keep, width, arrived, scale, features):
    per = keep.shape[1] // 2
    summed = scale is None
    out = struct((per, width), BF16)
    return pl.pallas_call(
        functools.partial(hidden_kernel, len(arrived), width, summed, features),
        out_shape=(out, struct((per, LANES), F32)) if summed else (out,),
        in_specs=[VMEM] * (1 + len(arrived) + (not summed)),
        out_specs=(VMEM,) * (1 + summed),
        name="hidden",
        compiler_params=pltpu.CompilerParams(vmem_limit_bytes=8 * MIB),
        cost_estimate=cost(keep.size * 10, keep.size * 10),
    )(keep, *arrived, *([] if summed else [scale]))


def join_kernel(*refs):
    sources, out_ref = refs[:-1], refs[-1]
    out_ref[...] = jnp.concatenate([ref[...].astype(F32) for ref in sources], axis=0).astype(BF16)


def join(parts):
    rows, width = parts[0].shape
    return pl.pallas_call(
        join_kernel,
        out_shape=struct((rows * len(parts), width), BF16),
        in_specs=[VMEM] * len(parts),
        out_specs=VMEM,
        name="join",
        compiler_params=pltpu.CompilerParams(vmem_limit_bytes=8 * MIB),
        cost_estimate=cost(0, rows * len(parts) * width * 4),
    )(*parts)


def down_kernel(first, count, added, fresh, base_ref, *refs):
    refs = list(refs)
    parts, weight, refs = refs[:count], refs[count], refs[count + 1 :]
    before = refs.pop(0) if added else None
    out_ref = refs.pop(0)
    if fresh:
        held, sems = refs
        row = pl.multiple_of(base_ref[0] + first, LANES)
        cuts = cuts_of(held.shape[0], 2 * PIECE)
        copies = start_copies([(weight.at[pl.ds(row + a, b - a), :], held.at[pl.ds(a, b - a), :]) for a, b in cuts], sems)
    else:
        held, cuts = weight, [(0, weight.shape[0])]
    hidden = jnp.concatenate([ref[...] for ref in parts], axis=0)
    total = before[...] if added else None
    for i, (a, b) in enumerate(cuts):
        if fresh:
            copies[i].wait()
        term = jnp.dot(hidden[:, a:b], held[a:b, :], preferred_element_type=F32)
        total = term if total is None else total + term
    out_ref[...] = total


def down(first, base, parts, weight, before, fresh):
    rows, width = sum(part.shape[0] for part in parts), weight.shape[1]
    depth = parts[0].shape[1]
    added = before is not None
    return pl.pallas_call(
        functools.partial(down_kernel, first, len(parts), added, fresh),
        out_shape=(struct((rows, width), F32),) + (struct((depth, width), BF16),) * fresh,
        in_specs=[SMEM] + [VMEM] * len(parts) + [HBM if fresh else VMEM] + [VMEM] * added,
        out_specs=(VMEM,) * (1 + fresh),
        scratch_shapes=[pltpu.SemaphoreType.DMA((len(cuts_of(depth, 2 * PIECE)),))] * fresh,
        name="down",
        compiler_params=pltpu.CompilerParams(vmem_limit_bytes=(DOWN_LIMIT if fresh else HELD_LIMIT) * MIB),
        cost_estimate=cost(2 * rows * depth * width, 2 * depth * width),
    )(base, *parts, weight, *([before] if added else []))


def chip_kernel(a_ref, b_ref, state_ref, state_out, send_ref):
    total = a_ref[...] + b_ref[...]
    send_ref[...] = total.astype(BF16)
    state_out[...] = state_ref[...] + total


def renew_kernel(state_ref, *refs):
    arrived, (state_out, x_ref, sumsq_ref) = refs[:-3], refs[-3:]
    state = state_ref[...]
    for ref in arrived:
        state = state + ref[...].astype(F32)
    state_out[...] = state
    x_ref[...] = state.astype(BF16)
    sumsq_ref[...] = rows_mean_square(state)


def finish_kernel(offsets, per, groups, where_ref, a_ref, b_ref, state_ref, out_ref, *refs):
    sends, (change, state) = refs[: groups - 1], refs[groups - 1 :]
    me, group = where_ref[0], where_ref[1]
    for p, offset in enumerate(offsets):
        first = (me ^ offset) * per
        if per % 8 == 0:
            first = pl.multiple_of(first, 8)
        rows = slice(p * per, (p + 1) * per)
        change[pl.ds(first, per), :] = a_ref[rows, :] + b_ref[rows, :]
        state[pl.ds(first, per), :] = state_ref[rows, :]
    rows = out_ref.shape[0]
    own = pl.ds(pl.multiple_of(group * rows, 8), rows)
    out_ref[...] = state[own, :] + change[own, :]
    for k, ref in enumerate(sends):
        other = pl.multiple_of(lax.rem(group + k + 1, groups) * rows, 8)
        ref[...] = change[pl.ds(other, rows), :].astype(BF16)


def per_device(counts, tokens, gate_weight, up_weight, down_weight):
    groups, wide, ffn = counts
    stages = stages_of(wide)
    offsets = offsets_of(stages)
    rows = tokens.shape[0] * groups
    per = rows // wide
    features = tokens.shape[1] * wide
    share = gate_weight.shape[1] // groups
    edges = [share // LANES * k // CHUNKS * LANES for k in range(CHUNKS + 1)]
    chunks = [(a, b - a) for a, b in zip(edges, edges[1:])]
    me, group = lax.axis_index("wide"), lax.axis_index("groups")
    where = jnp.stack([me, group]).astype(jnp.int32)
    base = (group * share).astype(jnp.int32).reshape(1)

    def from_group(value, k):
        return lax.ppermute(value, "groups", [((i + k) % groups, i) for i in range(groups)])

    others = [from_group(tokens, k) for k in range(1, groups)]
    state, x, sumsq = arrange(offsets, per, groups, where, tokens, others)

    def scatter_stage(low, size, sends):
        return [swap(send, "wide", i << low, wide) for i, send in zip(range(1, size), sends)]

    gates, downs = {}, {}
    gate_weight, up_weight, down_weight = (in_hbm(w) for w in (gate_weight, up_weight, down_weight))
    gates[0] = load(*chunks[0], base, gate_weight, up_weight)
    for step in range(STEPS):
        change = scale = None
        for c, (first, width) in enumerate(chunks):
            low, size = stages[0]
            fresh = c not in gates
            found = gate_up(
                first, width, per, size, base, x, sumsq if c == 0 else None,
                (gate_weight, up_weight) if fresh else gates[c], fresh,
            )
            keep, *sends = found[:size]
            if fresh:
                gates[c] = found[size:]
            arrived = scatter_stage(low, size, sends)
            for low, size in stages[1:]:
                keep, *sends = add_stage(keep, width, arrived, size)
                arrived = scatter_stage(low, size, sends)
            made = hidden_of(keep, width, arrived, scale, features)
            parts = [made[0]]
            if scale is None:
                scale = made[1]
            for low, size in reversed(stages):
                whole = parts[0] if len(parts) == 1 else join(parts)
                parts = [whole] + [swap(whole, "wide", i << low, wide) for i in range(1, size)]
            fresh = c not in downs
            found = down(first, base, parts, down_weight if fresh else downs[c], change, fresh)
            change = found[0]
            if fresh:
                downs[c] = found[1]
        other = swap(change, "ffn", 1, ffn)
        if step + 1 < STEPS:
            shape = state.shape
            state, send = pl.pallas_call(
                chip_kernel,
                out_shape=(struct(shape, F32), struct(shape, BF16)),
                in_specs=[VMEM] * 3,
                out_specs=(VMEM,) * 2,
                name="chip_sum",
                compiler_params=pltpu.CompilerParams(vmem_limit_bytes=8 * MIB),
                cost_estimate=cost(state.size, state.size * 16),
            )(change, other, state)
            arrived = [from_group(send, k) for k in range(1, groups)]
            state, x, sumsq = pl.pallas_call(
                renew_kernel,
                out_shape=(struct(shape, F32), struct(shape, BF16), struct((rows, LANES), F32)),
                in_specs=[VMEM] * (1 + len(arrived)),
                out_specs=(VMEM,) * 3,
                name="renew",
                compiler_params=pltpu.CompilerParams(vmem_limit_bytes=8 * MIB),
                cost_estimate=cost(state.size, state.size * 12),
            )(state, *arrived)
    own = struct(tokens.shape, F32)
    out, *sends = pl.pallas_call(
        functools.partial(finish_kernel, offsets, per, groups),
        out_shape=(own,) + (struct(tokens.shape, BF16),) * (groups - 1),
        in_specs=[SMEM] + [VMEM] * 3,
        out_specs=(VMEM,) * groups,
        scratch_shapes=[pltpu.VMEM(state.shape, F32)] * 2,
        name="finish",
        compiler_params=pltpu.CompilerParams(vmem_limit_bytes=8 * MIB),
        cost_estimate=cost(state.size, state.size * 16),
    )(where, change, other, state)
    for k, send in enumerate(sends):
        arrived = from_group(send, groups - 1 - k)
        out = out + arrived.astype(F32)
    return out


def solution(mesh):
    counts = tuple(mesh.shape[axis] for axis in ("groups", "wide", "ffn"))
    return jax.shard_map(
        functools.partial(per_device, counts),
        mesh=mesh,
        in_specs=(P("groups", "wide"), P("wide", "ffn"), P("wide", "ffn"), P("ffn", "wide")),
        out_specs=P("groups", "wide"),
        check_vma=False,
    )
```

```python
import functools

import jax
import jax.numpy as jnp
from jax import lax
from jax.experimental import pallas as pl
from jax.experimental.pallas import tpu as pltpu
from jax.sharding import PartitionSpec as P

STEPS = 2
CHUNKS = (27, 25)
SCATTER_BITS, GATHER_BITS = 2, 2
PRELOAD = True
TIE, PAIR = False, True
LANES = 128
PIECE = 256
F32 = jnp.float32
BF16 = jnp.bfloat16
SMEM = pl.BlockSpec(memory_space=pltpu.SMEM)
VMEM = pl.BlockSpec(memory_space=pltpu.VMEM)
HBM = pl.BlockSpec(memory_space=pltpu.HBM)
MIB = 2**20
LOAD_LIMIT, FRESH_LIMIT, DOWN_LIMIT, HELD_LIMIT = 10, 10, 10, 10


def struct(shape, dtype):
    return jax.ShapeDtypeStruct(shape, dtype)


def in_hbm(value):
    return pltpu.with_memory_space_constraint(value, pltpu.HBM)


def after(value, *earlier):
    return lax.optimization_barrier((value,) + earlier)[0]


def cost(flops, moved):
    return pl.CostEstimate(flops=int(flops), bytes_accessed=int(moved), transcendentals=0)


def stages_of(wide, most):
    found, low, total = [], 0, wide.bit_length() - 1
    while low < total:
        bits = min(most, total - low)
        found.append([reverse(i, bits) << low for i in range(1 << bits)])
        low += bits
    return found


def reverse(value, bits):
    return sum(((value >> k) & 1) << (bits - 1 - k) for k in range(bits))


def swap(value, axis, flip, count):
    return lax.ppermute(value, axis, [(i, i ^ flip) for i in range(count)])


def cuts_of(extent, piece):
    return [(a, min(a + piece, extent)) for a in range(0, extent, piece)]


def rows_mean_square(rows):
    total = jnp.sum(rows * rows, axis=1, keepdims=True)
    return jnp.broadcast_to(total, (rows.shape[0], LANES))


def arrange_kernel(offsets, per, groups, where_ref, own_ref, *refs):
    others, (state_ref, x_ref, sumsq_ref, whole) = refs[: groups - 1], refs[groups - 1 :]
    me, group = where_ref[0], where_ref[1]
    rows = own_ref.shape[0]
    for k, ref in enumerate((own_ref,) + tuple(others)):
        start = lax.rem(group + k, groups) * rows
        whole[pl.ds(pl.multiple_of(start, 8), rows), :] = ref[...].astype(F32)
    for p, offset in enumerate(offsets):
        first = (me ^ offset) * per
        if per % 8 == 0:
            first = pl.multiple_of(first, 8)
        state_ref[p * per : (p + 1) * per, :] = whole[pl.ds(first, per), :]
    state = state_ref[...]
    x_ref[...] = state.astype(BF16)
    sumsq_ref[...] = rows_mean_square(state)


def arrange(offsets, per, groups, where, own, others):
    rows, width = own.shape
    rows *= groups
    return pl.pallas_call(
        functools.partial(arrange_kernel, offsets, per, groups),
        out_shape=(struct((rows, width), F32), struct((rows, width), BF16), struct((rows, LANES), F32)),
        in_specs=[SMEM] + [VMEM] * groups,
        out_specs=(VMEM,) * 3,
        scratch_shapes=[pltpu.VMEM((rows, width), F32)],
        name="arrange",
        compiler_params=pltpu.CompilerParams(vmem_limit_bytes=8 * MIB),
        cost_estimate=cost(rows * width, rows * width * 10),
    )(where, own, *others)


def squeeze(value):
    return (value * jnp.abs(value)).astype(BF16)


def expand(ref, index=slice(None)):
    sent = ref[index].astype(F32)
    return sent * lax.rsqrt(jnp.maximum(jnp.abs(sent), 1e-37))


def three_lanes(value):
    shape = value.shape[:-1] + (LANES,)
    value = jnp.broadcast_to(value, shape)
    lane = lax.broadcasted_iota(jnp.int32, shape, len(shape) - 1)
    out = jnp.zeros(shape, F32)
    for k in range(3):
        part = value.astype(BF16).astype(F32)
        out = jnp.where(lane == k, part, out)
        value = value - part
    return out.astype(BF16)


def start_copies(pairs, sems):
    copies = [pltpu.make_async_copy(source, target, sems.at[i]) for i, (source, target) in enumerate(pairs)]
    for copy in copies:
        copy.start()
    return copies


def column_pairs(column, width, sources, targets):
    pairs = []
    for a, b in cuts_of(targets[0].shape[0], PIECE):
        for source, target in zip(sources, targets):
            pairs.append((source.at[pl.ds(a, b - a), pl.ds(column, width)], target.at[pl.ds(a, b - a), :]))
    return pairs


def load_kernel(first, base_ref, weight_hbm, held_ref, sems):
    column = pl.multiple_of(base_ref[0] + first, LANES)
    for copy in start_copies(column_pairs(column, held_ref.shape[1], (weight_hbm,), (held_ref,)), sems):
        copy.wait()


def load(first, width, base, weight):
    depth = weight.shape[0]
    return pl.pallas_call(
        functools.partial(load_kernel, first),
        out_shape=struct((depth, width), BF16),
        in_specs=[SMEM, HBM],
        out_specs=VMEM,
        scratch_shapes=[pltpu.SemaphoreType.DMA((len(cuts_of(depth, PIECE)),))],
        name="load",
        compiler_params=pltpu.CompilerParams(vmem_limit_bytes=LOAD_LIMIT * MIB),
        cost_estimate=cost(0, 4 * depth * width),
    )(base, weight)


def gate_up_kernel(first, per, size, fresh, summed, base_ref, x_ref, *refs):
    refs = list(refs)
    sumsq_ref = refs.pop(0) if summed else None
    weights, refs = refs[:2], refs[2:]
    outs, refs = refs[:size], refs[size:]
    column = pl.multiple_of(base_ref[0] + first, LANES)
    held, copies = [], []
    for k in range(2):
        target = refs.pop(0) if fresh[k] else weights[k]
        held.append(target)
        copies.append((weights[k], target) if fresh[k] else None)
    depth, width = held[0].shape
    cuts = cuts_of(depth, PIECE)
    for k in range(2):
        if fresh[k]:
            sems = refs.pop(0)
            copies[k] = start_copies(column_pairs(column, width, copies[k][:1], copies[k][1:]), sems)
    totals = [None, None]
    order = [(i, k) for i in range(len(cuts)) for k in range(2)]
    if fresh[0] != fresh[1]:
        order.sort(key=lambda one: fresh[one[1]])
    for i, k in order:
        a, b = cuts[i]
        if fresh[k]:
            copies[k][i].wait()
        term = jnp.dot(x_ref[:, a:b], held[k][a:b, :], preferred_element_type=F32)
        totals[k] = term if totals[k] is None else totals[k] + term
    group = outs[0].shape[0]
    for p in range(group * size):
        rows = slice(p * per, (p + 1) * per)
        both = jnp.concatenate([totals[0][rows], totals[1][rows]], axis=0)
        target = outs[p // group]
        target[p % group, :, :width] = both if p < group else squeeze(both)
        if summed:
            square = sumsq_ref[rows]
            square = jnp.concatenate([square, square], axis=0)
            target[p % group, :, width:] = square if p < group else three_lanes(square[:, :1])


def gate_up(first, width, per, size, base, x, sumsq, weights, fresh):
    rows, depth = x.shape
    group = rows // per // size
    summed = sumsq is not None
    shape = (group, 2 * per, width + LANES * summed)
    held = struct((depth, width), BF16)
    return pl.pallas_call(
        functools.partial(gate_up_kernel, first, per, size, fresh, summed),
        out_shape=(struct(shape, F32),) + (struct(shape, BF16),) * (size - 1) + (held,) * sum(fresh),
        in_specs=[SMEM, VMEM] + [VMEM] * summed + [HBM if one else VMEM for one in fresh],
        out_specs=(VMEM,) * (size + sum(fresh)),
        scratch_shapes=[pltpu.SemaphoreType.DMA((len(cuts_of(depth, PIECE)),))] * sum(fresh),
        name="gate_up",
        compiler_params=pltpu.CompilerParams(vmem_limit_bytes=(FRESH_LIMIT if any(fresh) else HELD_LIMIT) * MIB),
        cost_estimate=cost(4 * rows * depth * width, 4 * depth * width),
    )(base, x, *([sumsq] if summed else []), *weights)


def arrived_sum(keep, width, refs):
    total = keep[..., :width]
    for ref in refs:
        total = total + expand(ref, (slice(None), slice(None), slice(0, width)))
    if keep.shape[-1] == width:
        return total, None
    square = keep[..., width:]
    for ref in refs:
        square = square + jnp.sum(ref[:, :, width:].astype(F32), axis=-1, keepdims=True)
    return total, square


def add_kernel(count, width, pair, keep_ref, *refs):
    arrived, outs = refs[:count], refs[count:]
    total, square = arrived_sum(keep_ref[...], width, arrived)
    group = outs[0].shape[0]
    for i, out in enumerate(outs):
        rows = slice(None) if pair else slice(i * group, (i + 1) * group)
        out[:, :, :width] = total[rows] if i == 0 else squeeze(total[rows])
        if square is not None:
            out[:, :, width:] = square[rows] if i == 0 else three_lanes(square[rows][..., :1])


def add_stage(keep, width, arrived, size, pair):
    shape = (keep.shape[0] if pair else keep.shape[0] // size,) + keep.shape[1:]
    return pl.pallas_call(
        functools.partial(add_kernel, len(arrived), width, pair),
        out_shape=(struct(shape, F32),) + (struct(shape, BF16),) * (size - 1),
        in_specs=[VMEM] * (1 + len(arrived)),
        out_specs=(VMEM,) * size,
        name="add_partials",
        compiler_params=pltpu.CompilerParams(vmem_limit_bytes=8 * MIB),
        cost_estimate=cost(keep.size * 2, keep.size * 10),
    )(keep, *arrived)


def hidden_kernel(count, width, summed, features, pair, keep_ref, *refs):
    arrived, refs = refs[:count], refs[count:]
    out_ref = refs[0] if summed else refs[1]
    group = keep_ref.shape[0]
    per = keep_ref.shape[1] // 2
    made = []
    for p in range(group):
        total, square = arrived_sum(keep_ref[p : p + 1], width, [ref.at[pl.ds(group - 1 - p, 1)] for ref in arrived])
        total = total[0]
        rows = slice(p * per, (p + 1) * per)
        if summed:
            scale = 1.0 / jnp.sqrt(square[0][:per] / features + 1e-05)
            refs[1][rows] = scale
        else:
            scale = refs[0][rows]
        scale = scale[:, :1]
        gate, up = total[:per] * scale, total[per:] * scale
        made.append(gate / (1.0 + jnp.exp(-gate)) * up)
    out_ref[...] = jnp.concatenate(made, axis=0).astype(BF16)


def hidden_of(keep, width, arrived, scale, features, pair):
    group, both, _ = keep.shape
    rows = group * both // 2
    summed = scale is None
    out = struct((rows, width), BF16)
    return pl.pallas_call(
        functools.partial(hidden_kernel, len(arrived), width, summed, features, pair),
        out_shape=(out, struct((rows, LANES), F32)) if summed else (out,),
        in_specs=[VMEM] * (1 + len(arrived) + (not summed)),
        out_specs=(VMEM,) * (1 + summed),
        name="hidden",
        compiler_params=pltpu.CompilerParams(vmem_limit_bytes=8 * MIB),
        cost_estimate=cost(keep.size * 10, keep.size * 10),
    )(keep, *arrived, *([] if summed else [scale]))


def join_kernel(*refs):
    sources, out_ref = refs[:-1], refs[-1]
    out_ref[...] = jnp.concatenate([ref[...].astype(F32) for ref in sources], axis=0).astype(BF16)


def join(parts):
    rows, width = parts[0].shape
    return pl.pallas_call(
        join_kernel,
        out_shape=struct((rows * len(parts), width), BF16),
        in_specs=[VMEM] * len(parts),
        out_specs=VMEM,
        name="join",
        compiler_params=pltpu.CompilerParams(vmem_limit_bytes=8 * MIB),
        cost_estimate=cost(0, rows * len(parts) * width * 4),
    )(*parts)


def load_down_kernel(first, base_ref, down_hbm, after_ref, held, sems):
    row = pl.multiple_of(base_ref[0] + first, LANES)
    cuts = cuts_of(held.shape[0], 2 * PIECE)
    pairs = [(down_hbm.at[pl.ds(row + a, b - a), :], held.at[pl.ds(a, b - a), :]) for a, b in cuts]
    for copy in start_copies(pairs, sems):
        copy.wait()


def load_down(first, depth, base, weight, after):
    return pl.pallas_call(
        functools.partial(load_down_kernel, first),
        out_shape=struct((depth, weight.shape[1]), BF16),
        in_specs=[SMEM, HBM, VMEM],
        out_specs=VMEM,
        scratch_shapes=[pltpu.SemaphoreType.DMA((len(cuts_of(depth, 2 * PIECE)),))],
        name="load_down",
        compiler_params=pltpu.CompilerParams(vmem_limit_bytes=LOAD_LIMIT * MIB),
        cost_estimate=cost(0, 2 * depth * weight.shape[1]),
    )(base, weight, after)


def down_kernel(first, count, added, fresh, base_ref, *refs):
    refs = list(refs)
    parts, weight, refs = refs[:count], refs[count], refs[count + 1 :]
    before = refs.pop(0) if added else None
    out_ref = refs.pop(0)
    if fresh:
        held, sems = refs
        row = pl.multiple_of(base_ref[0] + first, LANES)
        cuts = cuts_of(held.shape[0], 2 * PIECE)
        copies = start_copies([(weight.at[pl.ds(row + a, b - a), :], held.at[pl.ds(a, b - a), :]) for a, b in cuts], sems)
    else:
        held, cuts = weight, [(0, weight.shape[0])]
    hidden = jnp.concatenate([ref[...] for ref in parts], axis=0)
    total = before[...] if added else None
    for i, (a, b) in enumerate(cuts):
        if fresh:
            copies[i].wait()
        term = jnp.dot(hidden[:, a:b], held[a:b, :], preferred_element_type=F32)
        total = term if total is None else total + term
    out_ref[...] = total


def down(first, base, parts, weight, before, fresh):
    rows, width = sum(part.shape[0] for part in parts), weight.shape[1]
    depth = parts[0].shape[1]
    added = before is not None
    return pl.pallas_call(
        functools.partial(down_kernel, first, len(parts), added, fresh),
        out_shape=(struct((rows, width), F32),) + (struct((depth, width), BF16),) * fresh,
        in_specs=[SMEM] + [VMEM] * len(parts) + [HBM if fresh else VMEM] + [VMEM] * added,
        out_specs=(VMEM,) * (1 + fresh),
        scratch_shapes=[pltpu.SemaphoreType.DMA((len(cuts_of(depth, 2 * PIECE)),))] * fresh,
        name="down",
        compiler_params=pltpu.CompilerParams(vmem_limit_bytes=(DOWN_LIMIT if fresh else HELD_LIMIT) * MIB),
        cost_estimate=cost(2 * rows * depth * width, 2 * depth * width),
    )(base, *parts, weight, *([before] if added else []))


def chip_kernel(a_ref, b_ref, state_ref, state_out, send_ref):
    total = a_ref[...] + b_ref[...]
    send_ref[...] = total.astype(BF16)
    state_out[...] = state_ref[...] + total


def renew_kernel(state_ref, *refs):
    arrived, (state_out, x_ref, sumsq_ref) = refs[:-3], refs[-3:]
    state = state_ref[...]
    for ref in arrived:
        state = state + ref[...].astype(F32)
    state_out[...] = state
    x_ref[...] = state.astype(BF16)
    sumsq_ref[...] = rows_mean_square(state)


def finish_kernel(offsets, per, groups, where_ref, a_ref, b_ref, state_ref, out_ref, *refs):
    sends, (change, state) = refs[: groups - 1], refs[groups - 1 :]
    me, group = where_ref[0], where_ref[1]
    for p, offset in enumerate(offsets):
        first = (me ^ offset) * per
        if per % 8 == 0:
            first = pl.multiple_of(first, 8)
        rows = slice(p * per, (p + 1) * per)
        change[pl.ds(first, per), :] = a_ref[rows, :] + b_ref[rows, :]
        state[pl.ds(first, per), :] = state_ref[rows, :]
    rows = out_ref.shape[0]
    own = pl.ds(pl.multiple_of(group * rows, 8), rows)
    out_ref[...] = state[own, :] + change[own, :]
    for k, ref in enumerate(sends):
        other = pl.multiple_of(lax.rem(group + k + 1, groups) * rows, 8)
        ref[...] = change[pl.ds(other, rows), :].astype(BF16)


def per_device(counts, tokens, gate_weight, up_weight, down_weight):
    groups, wide, ffn = counts
    stages, gathers = stages_of(wide, SCATTER_BITS), stages_of(wide, GATHER_BITS)
    offsets = [reverse(p, wide.bit_length() - 1) for p in range(wide)]
    rows = tokens.shape[0] * groups
    per = rows // wide
    features = tokens.shape[1] * wide
    share = gate_weight.shape[1] // groups
    edges = [share // LANES * sum(CHUNKS[:k]) // sum(CHUNKS) * LANES for k in range(len(CHUNKS) + 1)]
    chunks = [(a, b - a) for a, b in zip(edges, edges[1:])]
    me, group = lax.axis_index("wide"), lax.axis_index("groups")
    where = jnp.stack([me, group]).astype(jnp.int32)
    base = (group * share).astype(jnp.int32).reshape(1)

    def from_group(value, k):
        return lax.ppermute(value, "groups", [((i + k) % groups, i) for i in range(groups)])

    others = [from_group(tokens, k) for k in range(1, groups)]
    state, x, sumsq = arrange(offsets, per, groups, where, tokens, others)

    def scatter_stage(flips, sends):
        return [swap(send, "wide", flip, wide) for flip, send in zip(flips[1:], sends)]

    gate_weight, up_weight, down_weight = (in_hbm(w) for w in (gate_weight, up_weight, down_weight))
    last = len(chunks) - 1
    gates, downs = {}, {}
    early = load(*chunks[0], base, gate_weight)
    for step in range(STEPS):
        work, previous = [], x
        for c, (first, width) in enumerate(chunks):
            weights, fresh = gates.get(c, (gate_weight, up_weight)), (c not in gates,) * 2
            if fresh[0] and c == 0:
                weights, fresh = (early, up_weight), (False, True)
            size = len(stages[0])
            found = gate_up(
                first, width, per, size, base, after(x, previous), sumsq if c == 0 else None, weights, fresh
            )
            previous = found[0]
            if c not in gates:
                gates[c] = tuple(found[size:]) if c else (early, found[size])
            sends = list(found[1:size])
            if TIE and work:
                sends = [after(send, work[-1][1][0]) for send in sends]
            work.append((found[0], scatter_stage(stages[0], sends)))
        for at, flips in enumerate(stages[1:], 1):
            pair = PAIR and at + 1 == len(stages) and len(flips) == 2
            done = []
            for c, (first, width) in enumerate(chunks):
                keep, arrived = work[c]
                if c < last:
                    keep = after(keep, work[c + 1][0])
                elif c - 1 in downs and PRELOAD and step == 0:
                    keep = after(keep, downs[c - 1])
                keep, *sends = add_stage(keep, width, arrived, len(flips), pair)
                done.append((keep, scatter_stage(flips, sends)))
                if PRELOAD and c not in downs:
                    downs[c] = load_down(first, width, base, down_weight, keep)
            work = done
        scale, parts = None, []
        for c, (first, width) in enumerate(chunks):
            keep, arrived = work[c]
            if c < last:
                keep = after(keep, work[c + 1][0])
            elif c in downs:
                keep = after(keep, downs[c])
            made = hidden_of(keep, width, arrived, scale, features, pair)
            scale = made[1] if scale is None else scale
            parts.append([made[0]])
        for flips in reversed(gathers[:-1] if pair else gathers):
            done = []
            for c in range(len(chunks)):
                pieces = parts[c]
                if c < last and len(pieces) > 1:
                    pieces = [after(pieces[0], parts[c + 1][0])] + pieces[1:]
                done.append(pieces[0] if len(pieces) == 1 else join(pieces))
            for c in range(len(chunks)):
                whole = done[c]
                parts[c] = [whole] + [swap(whole, "wide", flip, wide) for flip in flips[1:]]
        change = None
        for c, (first, width) in enumerate(chunks):
            fresh = c not in downs
            if c < last:
                parts[c][0] = after(parts[c][0], parts[c + 1][0])
            found = down(first, base, parts[c], down_weight if fresh else downs[c], change, fresh)
            change = found[0]
            if fresh:
                downs[c] = found[1]
        other = swap(change, "ffn", 1, ffn)
        if step + 1 < STEPS:
            shape = state.shape
            state, send = pl.pallas_call(
                chip_kernel,
                out_shape=(struct(shape, F32), struct(shape, BF16)),
                in_specs=[VMEM] * 3,
                out_specs=(VMEM,) * 2,
                name="chip_sum",
                compiler_params=pltpu.CompilerParams(vmem_limit_bytes=8 * MIB),
                cost_estimate=cost(state.size, state.size * 16),
            )(change, other, state)
            arrived = [from_group(send, k) for k in range(1, groups)]
            state, x, sumsq = pl.pallas_call(
                renew_kernel,
                out_shape=(struct(shape, F32), struct(shape, BF16), struct((rows, LANES), F32)),
                in_specs=[VMEM] * (1 + len(arrived)),
                out_specs=(VMEM,) * 3,
                name="renew",
                compiler_params=pltpu.CompilerParams(vmem_limit_bytes=8 * MIB),
                cost_estimate=cost(state.size, state.size * 12),
            )(state, *arrived)
    own = struct(tokens.shape, F32)
    out, *sends = pl.pallas_call(
        functools.partial(finish_kernel, offsets, per, groups),
        out_shape=(own,) + (struct(tokens.shape, BF16),) * (groups - 1),
        in_specs=[SMEM] + [VMEM] * 3,
        out_specs=(VMEM,) * groups,
        scratch_shapes=[pltpu.VMEM(state.shape, F32)] * 2,
        name="finish",
        compiler_params=pltpu.CompilerParams(vmem_limit_bytes=8 * MIB),
        cost_estimate=cost(state.size, state.size * 16),
    )(where, change, other, state)
    for k, send in enumerate(sends):
        arrived = from_group(send, groups - 1 - k)
        out = out + arrived.astype(F32)
    return out


def solution(mesh):
    counts = tuple(mesh.shape[axis] for axis in ("groups", "wide", "ffn"))
    return jax.shard_map(
        functools.partial(per_device, counts),
        mesh=mesh,
        in_specs=(P("groups", "wide"), P("wide", "ffn"), P("wide", "ffn"), P("ffn", "wide")),
        out_specs=P("groups", "wide"),
        check_vma=False,
    )
```

```python
import functools

import jax
import jax.numpy as jnp
from jax import lax
from jax.experimental import pallas as pl
from jax.experimental.pallas import tpu as pltpu
from jax.sharding import PartitionSpec as P

STEPS = 2
CHUNKS = (27, 25)
SCATTER_BITS, GATHER_BITS = 2, 2
PRELOAD = True
TIE, PAIR = False, True
LANES = 128
PIECE = 256
F32 = jnp.float32
BF16 = jnp.bfloat16
SMEM = pl.BlockSpec(memory_space=pltpu.SMEM)
VMEM = pl.BlockSpec(memory_space=pltpu.VMEM)
HBM = pl.BlockSpec(memory_space=pltpu.HBM)
MIB = 2**20
LOAD_LIMIT, FRESH_LIMIT, DOWN_LIMIT, HELD_LIMIT = 10, 10, 10, 10


def struct(shape, dtype):
    return jax.ShapeDtypeStruct(shape, dtype)


def in_hbm(value):
    return pltpu.with_memory_space_constraint(value, pltpu.HBM)


def after(value, *earlier):
    return lax.optimization_barrier((value,) + earlier)[0]


def cost(flops, moved):
    return pl.CostEstimate(flops=int(flops), bytes_accessed=int(moved), transcendentals=0)


def stages_of(wide, most):
    found, low, total = [], 0, wide.bit_length() - 1
    while low < total:
        bits = min(most, total - low)
        found.append([reverse(i, bits) << low for i in range(1 << bits)])
        low += bits
    return found


def reverse(value, bits):
    return sum(((value >> k) & 1) << (bits - 1 - k) for k in range(bits))


def swap(value, axis, flip, count):
    return lax.ppermute(value, axis, [(i, i ^ flip) for i in range(count)])


def cuts_of(extent, piece):
    return [(a, min(a + piece, extent)) for a in range(0, extent, piece)]


def rows_mean_square(rows):
    total = jnp.sum(rows * rows, axis=1, keepdims=True)
    return jnp.broadcast_to(total, (rows.shape[0], LANES))


def arrange_kernel(offsets, per, groups, where_ref, own_ref, *refs):
    others, (state_ref, x_ref, sumsq_ref, whole) = refs[: groups - 1], refs[groups - 1 :]
    me, group = where_ref[0], where_ref[1]
    rows = own_ref.shape[0]
    for k, ref in enumerate((own_ref,) + tuple(others)):
        start = lax.rem(group + k, groups) * rows
        whole[pl.ds(pl.multiple_of(start, 8), rows), :] = ref[...].astype(F32)
    for p, offset in enumerate(offsets):
        first = (me ^ offset) * per
        if per % 8 == 0:
            first = pl.multiple_of(first, 8)
        state_ref[p * per : (p + 1) * per, :] = whole[pl.ds(first, per), :]
    state = state_ref[...]
    x_ref[...] = state.astype(BF16)
    sumsq_ref[...] = rows_mean_square(state)


def arrange(offsets, per, groups, where, own, others):
    rows, width = own.shape
    rows *= groups
    return pl.pallas_call(
        functools.partial(arrange_kernel, offsets, per, groups),
        out_shape=(struct((rows, width), F32), struct((rows, width), BF16), struct((rows, LANES), F32)),
        in_specs=[SMEM] + [VMEM] * groups,
        out_specs=(VMEM,) * 3,
        scratch_shapes=[pltpu.VMEM((rows, width), F32)],
        name="arrange",
        compiler_params=pltpu.CompilerParams(vmem_limit_bytes=8 * MIB),
        cost_estimate=cost(rows * width, rows * width * 10),
    )(where, own, *others)


def squeeze(value):
    return (value * jnp.abs(value)).astype(BF16)


def expand(ref, index=slice(None)):
    sent = ref[index].astype(F32)
    return sent * lax.rsqrt(jnp.maximum(jnp.abs(sent), 1e-37))


def three_lanes(value):
    shape = value.shape[:-1] + (LANES,)
    value = jnp.broadcast_to(value, shape)
    lane = lax.broadcasted_iota(jnp.int32, shape, len(shape) - 1)
    out = jnp.zeros(shape, F32)
    for k in range(3):
        part = value.astype(BF16).astype(F32)
        out = jnp.where(lane == k, part, out)
        value = value - part
    return out.astype(BF16)


def start_copies(pairs, sems):
    copies = [pltpu.make_async_copy(source, target, sems.at[i]) for i, (source, target) in enumerate(pairs)]
    for copy in copies:
        copy.start()
    return copies


def column_pairs(column, width, sources, targets):
    pairs = []
    for a, b in cuts_of(targets[0].shape[0], PIECE):
        for source, target in zip(sources, targets):
            pairs.append((source.at[pl.ds(a, b - a), pl.ds(column, width)], target.at[pl.ds(a, b - a), :]))
    return pairs


def load_kernel(first, base_ref, weight_hbm, held_ref, sems):
    column = pl.multiple_of(base_ref[0] + first, LANES)
    for copy in start_copies(column_pairs(column, held_ref.shape[1], (weight_hbm,), (held_ref,)), sems):
        copy.wait()


def load(first, width, base, weight):
    depth = weight.shape[0]
    return pl.pallas_call(
        functools.partial(load_kernel, first),
        out_shape=struct((depth, width), BF16),
        in_specs=[SMEM, HBM],
        out_specs=VMEM,
        scratch_shapes=[pltpu.SemaphoreType.DMA((len(cuts_of(depth, PIECE)),))],
        name="load",
        compiler_params=pltpu.CompilerParams(vmem_limit_bytes=LOAD_LIMIT * MIB),
        cost_estimate=cost(0, 4 * depth * width),
    )(base, weight)


def gate_up_kernel(first, per, size, fresh, summed, base_ref, x_ref, *refs):
    refs = list(refs)
    sumsq_ref = refs.pop(0) if summed else None
    weights, refs = refs[:2], refs[2:]
    outs, refs = refs[:size], refs[size:]
    column = pl.multiple_of(base_ref[0] + first, LANES)
    held, copies = [], []
    for k in range(2):
        target = refs.pop(0) if fresh[k] else weights[k]
        held.append(target)
        copies.append((weights[k], target) if fresh[k] else None)
    depth, width = held[0].shape
    cuts = cuts_of(depth, PIECE)
    for k in range(2):
        if fresh[k]:
            sems = refs.pop(0)
            copies[k] = start_copies(column_pairs(column, width, copies[k][:1], copies[k][1:]), sems)
    totals = [None, None]
    order = [(i, k) for i in range(len(cuts)) for k in range(2)]
    if fresh[0] != fresh[1]:
        order.sort(key=lambda one: fresh[one[1]])
    for i, k in order:
        a, b = cuts[i]
        if fresh[k]:
            copies[k][i].wait()
        term = jnp.dot(x_ref[:, a:b], held[k][a:b, :], preferred_element_type=F32)
        totals[k] = term if totals[k] is None else totals[k] + term
    group = outs[0].shape[0]
    for p in range(group * size):
        rows = slice(p * per, (p + 1) * per)
        both = jnp.concatenate([totals[0][rows], totals[1][rows]], axis=0)
        target = outs[p // group]
        target[p % group, :, :width] = both if p < group else squeeze(both)
        if summed:
            square = sumsq_ref[rows]
            square = jnp.concatenate([square, square], axis=0)
            target[p % group, :, width:] = square if p < group else three_lanes(square[:, :1])


def gate_up(first, width, per, size, base, x, sumsq, weights, fresh):
    rows, depth = x.shape
    group = rows // per // size
    summed = sumsq is not None
    shape = (group, 2 * per, width + LANES * summed)
    held = struct((depth, width), BF16)
    return pl.pallas_call(
        functools.partial(gate_up_kernel, first, per, size, fresh, summed),
        out_shape=(struct(shape, F32),) + (struct(shape, BF16),) * (size - 1) + (held,) * sum(fresh),
        in_specs=[SMEM, VMEM] + [VMEM] * summed + [HBM if one else VMEM for one in fresh],
        out_specs=(VMEM,) * (size + sum(fresh)),
        scratch_shapes=[pltpu.SemaphoreType.DMA((len(cuts_of(depth, PIECE)),))] * sum(fresh),
        name="gate_up",
        compiler_params=pltpu.CompilerParams(vmem_limit_bytes=(FRESH_LIMIT if any(fresh) else HELD_LIMIT) * MIB),
        cost_estimate=cost(4 * rows * depth * width, 4 * depth * width),
    )(base, x, *([sumsq] if summed else []), *weights)


def arrived_sum(keep, width, refs):
    total = keep[..., :width]
    for ref in refs:
        total = total + expand(ref, (slice(None), slice(None), slice(0, width)))
    if keep.shape[-1] == width:
        return total, None
    square = keep[..., width:]
    for ref in refs:
        square = square + jnp.sum(ref[:, :, width:].astype(F32), axis=-1, keepdims=True)
    return total, square


def add_kernel(count, width, pair, keep_ref, *refs):
    arrived, outs = refs[:count], refs[count:]
    total, square = arrived_sum(keep_ref[...], width, arrived)
    group = outs[0].shape[0]
    for i, out in enumerate(outs):
        rows = slice(None) if pair else slice(i * group, (i + 1) * group)
        out[:, :, :width] = total[rows] if i == 0 else squeeze(total[rows])
        if square is not None:
            out[:, :, width:] = square[rows] if i == 0 else three_lanes(square[rows][..., :1])


def add_stage(keep, width, arrived, size, pair):
    shape = (keep.shape[0] if pair else keep.shape[0] // size,) + keep.shape[1:]
    return pl.pallas_call(
        functools.partial(add_kernel, len(arrived), width, pair),
        out_shape=(struct(shape, F32),) + (struct(shape, BF16),) * (size - 1),
        in_specs=[VMEM] * (1 + len(arrived)),
        out_specs=(VMEM,) * size,
        name="add_partials",
        compiler_params=pltpu.CompilerParams(vmem_limit_bytes=8 * MIB),
        cost_estimate=cost(keep.size * 2, keep.size * 10),
    )(keep, *arrived)


def hidden_kernel(count, width, summed, features, pair, keep_ref, *refs):
    arrived, refs = refs[:count], refs[count:]
    out_ref = refs[0] if summed else refs[1]
    group = keep_ref.shape[0]
    per = keep_ref.shape[1] // 2
    made = []
    for p in range(group):
        total, square = arrived_sum(keep_ref[p : p + 1], width, [ref.at[pl.ds(group - 1 - p, 1)] for ref in arrived])
        total = total[0]
        rows = slice(p * per, (p + 1) * per)
        if summed:
            scale = 1.0 / jnp.sqrt(square[0][:per] / features + 1e-05)
            refs[1][rows] = scale
        else:
            scale = refs[0][rows]
        scale = scale[:, :1]
        gate, up = total[:per] * scale, total[per:] * scale
        made.append(gate / (1.0 + jnp.exp(-gate)) * up)
    out_ref[...] = jnp.concatenate(made, axis=0).astype(BF16)


def hidden_of(keep, width, arrived, scale, features, pair):
    group, both, _ = keep.shape
    rows = group * both // 2
    summed = scale is None
    out = struct((rows, width), BF16)
    return pl.pallas_call(
        functools.partial(hidden_kernel, len(arrived), width, summed, features, pair),
        out_shape=(out, struct((rows, LANES), F32)) if summed else (out,),
        in_specs=[VMEM] * (1 + len(arrived) + (not summed)),
        out_specs=(VMEM,) * (1 + summed),
        name="hidden",
        compiler_params=pltpu.CompilerParams(vmem_limit_bytes=8 * MIB),
        cost_estimate=cost(keep.size * 10, keep.size * 10),
    )(keep, *arrived, *([] if summed else [scale]))


def join_kernel(*refs):
    sources, out_ref = refs[:-1], refs[-1]
    out_ref[...] = jnp.concatenate([ref[...].astype(F32) for ref in sources], axis=0).astype(BF16)


def join(parts):
    rows, width = parts[0].shape
    return pl.pallas_call(
        join_kernel,
        out_shape=struct((rows * len(parts), width), BF16),
        in_specs=[VMEM] * len(parts),
        out_specs=VMEM,
        name="join",
        compiler_params=pltpu.CompilerParams(vmem_limit_bytes=8 * MIB),
        cost_estimate=cost(0, rows * len(parts) * width * 4),
    )(*parts)


def load_down_kernel(first, base_ref, down_hbm, after_ref, held, sems):
    row = pl.multiple_of(base_ref[0] + first, LANES)
    cuts = cuts_of(held.shape[0], 2 * PIECE)
    pairs = [(down_hbm.at[pl.ds(row + a, b - a), :], held.at[pl.ds(a, b - a), :]) for a, b in cuts]
    for copy in start_copies(pairs, sems):
        copy.wait()


def load_down(first, depth, base, weight, after):
    return pl.pallas_call(
        functools.partial(load_down_kernel, first),
        out_shape=struct((depth, weight.shape[1]), BF16),
        in_specs=[SMEM, HBM, VMEM],
        out_specs=VMEM,
        scratch_shapes=[pltpu.SemaphoreType.DMA((len(cuts_of(depth, 2 * PIECE)),))],
        name="load_down",
        compiler_params=pltpu.CompilerParams(vmem_limit_bytes=LOAD_LIMIT * MIB),
        cost_estimate=cost(0, 2 * depth * weight.shape[1]),
    )(base, weight, after)


def down_kernel(first, count, added, fresh, sent, base_ref, *refs):
    refs = list(refs)
    parts, weight, refs = refs[:count], refs[count], refs[count + 1 :]
    before = refs.pop(0) if added else None
    out_ref = refs.pop(0)
    send_ref = refs.pop(0) if sent else None
    if fresh:
        held, sems = refs
        row = pl.multiple_of(base_ref[0] + first, LANES)
        cuts = cuts_of(held.shape[0], 2 * PIECE)
        copies = start_copies([(weight.at[pl.ds(row + a, b - a), :], held.at[pl.ds(a, b - a), :]) for a, b in cuts], sems)
    else:
        held, cuts = weight, [(0, weight.shape[0])]
    hidden = jnp.concatenate([ref[...] for ref in parts], axis=0)
    total = before[...] if added else None
    for i, (a, b) in enumerate(cuts):
        if fresh:
            copies[i].wait()
        term = jnp.dot(hidden[:, a:b], held[a:b, :], preferred_element_type=F32)
        total = term if total is None else total + term
    out_ref[...] = total
    if sent:
        send_ref[...] = total.astype(BF16)


def down(first, base, parts, weight, before, fresh, sent):
    rows, width = sum(part.shape[0] for part in parts), weight.shape[1]
    depth = parts[0].shape[1]
    added = before is not None
    return pl.pallas_call(
        functools.partial(down_kernel, first, len(parts), added, fresh, sent),
        out_shape=(struct((rows, width), F32),)
        + (struct((rows, width), BF16),) * sent
        + (struct((depth, width), BF16),) * fresh,
        in_specs=[SMEM] + [VMEM] * len(parts) + [HBM if fresh else VMEM] + [VMEM] * added,
        out_specs=(VMEM,) * (1 + sent + fresh),
        scratch_shapes=[pltpu.SemaphoreType.DMA((len(cuts_of(depth, 2 * PIECE)),))] * fresh,
        name="down",
        compiler_params=pltpu.CompilerParams(vmem_limit_bytes=(DOWN_LIMIT if fresh else HELD_LIMIT) * MIB),
        cost_estimate=cost(2 * rows * depth * width, 2 * depth * width),
    )(base, *parts, weight, *([before] if added else []))


def chip_kernel(a_ref, b_ref, state_ref, state_out, send_ref):
    total = a_ref[...] + b_ref[...].astype(F32)
    send_ref[...] = total.astype(BF16)
    state_out[...] = state_ref[...] + total


def renew_kernel(state_ref, *refs):
    arrived, (state_out, x_ref, sumsq_ref) = refs[:-3], refs[-3:]
    state = state_ref[...]
    for ref in arrived:
        state = state + ref[...].astype(F32)
    state_out[...] = state
    x_ref[...] = state.astype(BF16)
    sumsq_ref[...] = rows_mean_square(state)


def finish_kernel(offsets, per, groups, where_ref, a_ref, b_ref, state_ref, out_ref, *refs):
    sends, (change, state) = refs[: groups - 1], refs[groups - 1 :]
    me, group = where_ref[0], where_ref[1]
    other = b_ref[...].astype(F32)
    for p, offset in enumerate(offsets):
        first = (me ^ offset) * per
        if per % 8 == 0:
            first = pl.multiple_of(first, 8)
        rows = slice(p * per, (p + 1) * per)
        change[pl.ds(first, per), :] = a_ref[rows, :] + other[rows, :]
        state[pl.ds(first, per), :] = state_ref[rows, :]
    rows = out_ref.shape[0]
    own = pl.ds(pl.multiple_of(group * rows, 8), rows)
    out_ref[...] = state[own, :] + change[own, :]
    for k, ref in enumerate(sends):
        other = pl.multiple_of(lax.rem(group + k + 1, groups) * rows, 8)
        ref[...] = change[pl.ds(other, rows), :].astype(BF16)


def per_device(counts, tokens, gate_weight, up_weight, down_weight):
    groups, wide, ffn = counts
    stages, gathers = stages_of(wide, SCATTER_BITS), stages_of(wide, GATHER_BITS)
    offsets = [reverse(p, wide.bit_length() - 1) for p in range(wide)]
    rows = tokens.shape[0] * groups
    per = rows // wide
    features = tokens.shape[1] * wide
    share = gate_weight.shape[1] // groups
    edges = [share // LANES * sum(CHUNKS[:k]) // sum(CHUNKS) * LANES for k in range(len(CHUNKS) + 1)]
    chunks = [(a, b - a) for a, b in zip(edges, edges[1:])]
    me, group = lax.axis_index("wide"), lax.axis_index("groups")
    where = jnp.stack([me, group]).astype(jnp.int32)
    base = (group * share).astype(jnp.int32).reshape(1)

    def from_group(value, k):
        return lax.ppermute(value, "groups", [((i + k) % groups, i) for i in range(groups)])

    others = [from_group(tokens, k) for k in range(1, groups)]
    state, x, sumsq = arrange(offsets, per, groups, where, tokens, others)

    def scatter_stage(flips, sends):
        return [swap(send, "wide", flip, wide) for flip, send in zip(flips[1:], sends)]

    gate_weight, up_weight, down_weight = (in_hbm(w) for w in (gate_weight, up_weight, down_weight))
    last = len(chunks) - 1
    gates, downs = {}, {}
    early = load(*chunks[0], base, gate_weight)
    for step in range(STEPS):
        work, previous = [], x
        for c, (first, width) in enumerate(chunks):
            weights, fresh = gates.get(c, (gate_weight, up_weight)), (c not in gates,) * 2
            if fresh[0] and c == 0:
                weights, fresh = (early, up_weight), (False, True)
            size = len(stages[0])
            found = gate_up(
                first, width, per, size, base, after(x, previous), sumsq if c == 0 else None, weights, fresh
            )
            previous = found[0]
            if c not in gates:
                gates[c] = tuple(found[size:]) if c else (early, found[size])
            sends = list(found[1:size])
            if TIE and work:
                sends = [after(send, work[-1][1][0]) for send in sends]
            work.append((found[0], scatter_stage(stages[0], sends)))
        for at, flips in enumerate(stages[1:], 1):
            pair = PAIR and at + 1 == len(stages) and len(flips) == 2
            done = []
            for c, (first, width) in enumerate(chunks):
                keep, arrived = work[c]
                if c < last:
                    keep = after(keep, work[c + 1][0])
                elif c - 1 in downs and PRELOAD and step == 0:
                    keep = after(keep, downs[c - 1])
                keep, *sends = add_stage(keep, width, arrived, len(flips), pair)
                done.append((keep, scatter_stage(flips, sends)))
                if PRELOAD and c not in downs:
                    downs[c] = load_down(first, width, base, down_weight, keep)
            work = done
        scale, parts = None, []
        for c, (first, width) in enumerate(chunks):
            keep, arrived = work[c]
            if c < last:
                keep = after(keep, work[c + 1][0])
            elif c in downs:
                keep = after(keep, downs[c])
            made = hidden_of(keep, width, arrived, scale, features, pair)
            scale = made[1] if scale is None else scale
            parts.append([made[0]])
        for flips in reversed(gathers[:-1] if pair else gathers):
            done = []
            for c in range(len(chunks)):
                pieces = parts[c]
                if c < last and len(pieces) > 1:
                    pieces = [after(pieces[0], parts[c + 1][0])] + pieces[1:]
                done.append(pieces[0] if len(pieces) == 1 else join(pieces))
            for c in range(len(chunks)):
                whole = done[c]
                parts[c] = [whole] + [swap(whole, "wide", flip, wide) for flip in flips[1:]]
        change = None
        for c, (first, width) in enumerate(chunks):
            fresh = c not in downs
            if c < last:
                parts[c][0] = after(parts[c][0], parts[c + 1][0])
            found = down(first, base, parts[c], down_weight if fresh else downs[c], change, fresh, c == last)
            change = found[0]
            if fresh:
                downs[c] = found[-1]
        other = swap(found[1], "ffn", 1, ffn)
        if step + 1 < STEPS:
            shape = state.shape
            state, send = pl.pallas_call(
                chip_kernel,
                out_shape=(struct(shape, F32), struct(shape, BF16)),
                in_specs=[VMEM] * 3,
                out_specs=(VMEM,) * 2,
                name="chip_sum",
                compiler_params=pltpu.CompilerParams(vmem_limit_bytes=8 * MIB),
                cost_estimate=cost(state.size, state.size * 16),
            )(change, other, state)
            arrived = [from_group(send, k) for k in range(1, groups)]
            state, x, sumsq = pl.pallas_call(
                renew_kernel,
                out_shape=(struct(shape, F32), struct(shape, BF16), struct((rows, LANES), F32)),
                in_specs=[VMEM] * (1 + len(arrived)),
                out_specs=(VMEM,) * 3,
                name="renew",
                compiler_params=pltpu.CompilerParams(vmem_limit_bytes=8 * MIB),
                cost_estimate=cost(state.size, state.size * 12),
            )(state, *arrived)
    own = struct(tokens.shape, F32)
    out, *sends = pl.pallas_call(
        functools.partial(finish_kernel, offsets, per, groups),
        out_shape=(own,) + (struct(tokens.shape, BF16),) * (groups - 1),
        in_specs=[SMEM] + [VMEM] * 3,
        out_specs=(VMEM,) * groups,
        scratch_shapes=[pltpu.VMEM(state.shape, F32)] * 2,
        name="finish",
        compiler_params=pltpu.CompilerParams(vmem_limit_bytes=8 * MIB),
        cost_estimate=cost(state.size, state.size * 16),
    )(where, change, other, state)
    for k, send in enumerate(sends):
        arrived = from_group(send, groups - 1 - k)
        out = out + arrived.astype(F32)
    return out


def solution(mesh):
    counts = tuple(mesh.shape[axis] for axis in ("groups", "wide", "ffn"))
    return jax.shard_map(
        functools.partial(per_device, counts),
        mesh=mesh,
        in_specs=(P("groups", "wide"), P("wide", "ffn"), P("wide", "ffn"), P("ffn", "wide")),
        out_specs=P("groups", "wide"),
        check_vma=False,
    )
```

```python
import functools

import jax
import jax.numpy as jnp
from jax import lax
from jax.experimental import pallas as pl
from jax.experimental.pallas import tpu as pltpu
from jax.sharding import PartitionSpec as P

STEPS = 2
CHUNKS = (27, 25)
SCATTER_BITS, GATHER_BITS = 2, 2
PRELOAD = True
TIE, PAIR = False, True
LANES = 128
PIECE = 256
F32 = jnp.float32
BF16 = jnp.bfloat16
SMEM = pl.BlockSpec(memory_space=pltpu.SMEM)
VMEM = pl.BlockSpec(memory_space=pltpu.VMEM)
HBM = pl.BlockSpec(memory_space=pltpu.HBM)
MIB = 2**20
LOAD_LIMIT, FRESH_LIMIT, DOWN_LIMIT, HELD_LIMIT = 10, 10, 10, 10


def struct(shape, dtype):
    return jax.ShapeDtypeStruct(shape, dtype)


def in_hbm(value):
    return pltpu.with_memory_space_constraint(value, pltpu.HBM)


def after(value, *earlier):
    return lax.optimization_barrier((value,) + earlier)[0]


def cost(flops, moved):
    return pl.CostEstimate(flops=int(flops), bytes_accessed=int(moved), transcendentals=0)


def stages_of(wide, most):
    found, low, total = [], 0, wide.bit_length() - 1
    while low < total:
        bits = min(most, total - low)
        found.append([reverse(i, bits) << low for i in range(1 << bits)])
        low += bits
    return found


def reverse(value, bits):
    return sum(((value >> k) & 1) << (bits - 1 - k) for k in range(bits))


def swap(value, axis, flip, count):
    return lax.ppermute(value, axis, [(i, i ^ flip) for i in range(count)])


def cuts_of(extent, piece):
    return [(a, min(a + piece, extent)) for a in range(0, extent, piece)]


def rows_mean_square(rows):
    total = jnp.sum(rows * rows, axis=1, keepdims=True)
    return jnp.broadcast_to(total, (rows.shape[0], LANES))


def arrange_kernel(offsets, per, groups, where_ref, own_ref, *refs):
    others, (state_ref, x_ref, sumsq_ref, whole) = refs[: groups - 1], refs[groups - 1 :]
    me, group = where_ref[0], where_ref[1]
    rows = own_ref.shape[0]
    for k, ref in enumerate((own_ref,) + tuple(others)):
        start = lax.rem(group + k, groups) * rows
        whole[pl.ds(pl.multiple_of(start, 8), rows), :] = ref[...].astype(F32)
    for p, offset in enumerate(offsets):
        first = (me ^ offset) * per
        if per % 8 == 0:
            first = pl.multiple_of(first, 8)
        state_ref[p * per : (p + 1) * per, :] = whole[pl.ds(first, per), :]
    state = state_ref[...]
    x_ref[...] = state.astype(BF16)
    sumsq_ref[...] = rows_mean_square(state)


def arrange(offsets, per, groups, where, own, others):
    rows, width = own.shape
    rows *= groups
    return pl.pallas_call(
        functools.partial(arrange_kernel, offsets, per, groups),
        out_shape=(struct((rows, width), F32), struct((rows, width), BF16), struct((rows, LANES), F32)),
        in_specs=[SMEM] + [VMEM] * groups,
        out_specs=(VMEM,) * 3,
        scratch_shapes=[pltpu.VMEM((rows, width), F32)],
        name="arrange",
        compiler_params=pltpu.CompilerParams(vmem_limit_bytes=8 * MIB),
        cost_estimate=cost(rows * width, rows * width * 10),
    )(where, own, *others)


def squeeze(value):
    return (value * jnp.abs(value)).astype(BF16)


def expand(ref, index=slice(None)):
    sent = ref[index].astype(F32)
    return sent * lax.rsqrt(jnp.maximum(jnp.abs(sent), 1e-37))


def three_lanes(value):
    shape = value.shape[:-1] + (LANES,)
    value = jnp.broadcast_to(value, shape)
    lane = lax.broadcasted_iota(jnp.int32, shape, len(shape) - 1)
    out = jnp.zeros(shape, F32)
    for k in range(3):
        part = value.astype(BF16).astype(F32)
        out = jnp.where(lane == k, part, out)
        value = value - part
    return out.astype(BF16)


def start_copies(pairs, sems):
    copies = [pltpu.make_async_copy(source, target, sems.at[i]) for i, (source, target) in enumerate(pairs)]
    for copy in copies:
        copy.start()
    return copies


def column_pairs(column, width, sources, targets):
    pairs = []
    for a, b in cuts_of(targets[0].shape[0], PIECE):
        for source, target in zip(sources, targets):
            pairs.append((source.at[pl.ds(a, b - a), pl.ds(column, width)], target.at[pl.ds(a, b - a), :]))
    return pairs


def load_kernel(first, base_ref, weight_hbm, held_ref, sems):
    column = pl.multiple_of(base_ref[0] + first, LANES)
    for copy in start_copies(column_pairs(column, held_ref.shape[1], (weight_hbm,), (held_ref,)), sems):
        copy.wait()


def load(first, width, base, weight):
    depth = weight.shape[0]
    return pl.pallas_call(
        functools.partial(load_kernel, first),
        out_shape=struct((depth, width), BF16),
        in_specs=[SMEM, HBM],
        out_specs=VMEM,
        scratch_shapes=[pltpu.SemaphoreType.DMA((len(cuts_of(depth, PIECE)),))],
        name="load",
        compiler_params=pltpu.CompilerParams(vmem_limit_bytes=LOAD_LIMIT * MIB),
        cost_estimate=cost(0, 4 * depth * width),
    )(base, weight)


def gate_up_kernel(first, per, size, fresh, summed, base_ref, x_ref, *refs):
    refs = list(refs)
    sumsq_ref = refs.pop(0) if summed else None
    weights, refs = refs[:2], refs[2:]
    outs, refs = refs[:size], refs[size:]
    column = pl.multiple_of(base_ref[0] + first, LANES)
    held, copies = [], []
    for k in range(2):
        target = refs.pop(0) if fresh[k] else weights[k]
        held.append(target)
        copies.append((weights[k], target) if fresh[k] else None)
    depth, width = held[0].shape
    cuts = cuts_of(depth, PIECE)
    for k in range(2):
        if fresh[k]:
            sems = refs.pop(0)
            copies[k] = start_copies(column_pairs(column, width, copies[k][:1], copies[k][1:]), sems)
    totals = [None, None]
    order = [(i, k) for i in range(len(cuts)) for k in range(2)]
    if fresh[0] != fresh[1]:
        order.sort(key=lambda one: fresh[one[1]])
    for i, k in order:
        a, b = cuts[i]
        if fresh[k]:
            copies[k][i].wait()
        term = jnp.dot(x_ref[:, a:b], held[k][a:b, :], preferred_element_type=F32)
        totals[k] = term if totals[k] is None else totals[k] + term
    group = outs[0].shape[0]
    for p in range(group * size):
        rows = slice(p * per, (p + 1) * per)
        both = jnp.concatenate([totals[0][rows], totals[1][rows]], axis=0)
        target = outs[p // group]
        target[p % group, :, :width] = both if p < group else squeeze(both)
        if summed:
            square = sumsq_ref[rows]
            square = jnp.concatenate([square, square], axis=0)
            target[p % group, :, width:] = square if p < group else three_lanes(square[:, :1])


def gate_up(first, width, per, size, base, x, sumsq, weights, fresh):
    rows, depth = x.shape
    group = rows // per // size
    summed = sumsq is not None
    shape = (group, 2 * per, width + LANES * summed)
    held = struct((depth, width), BF16)
    return pl.pallas_call(
        functools.partial(gate_up_kernel, first, per, size, fresh, summed),
        out_shape=(struct(shape, F32),) + (struct(shape, BF16),) * (size - 1) + (held,) * sum(fresh),
        in_specs=[SMEM, VMEM] + [VMEM] * summed + [HBM if one else VMEM for one in fresh],
        out_specs=(VMEM,) * (size + sum(fresh)),
        scratch_shapes=[pltpu.SemaphoreType.DMA((len(cuts_of(depth, PIECE)),))] * sum(fresh),
        name="gate_up",
        compiler_params=pltpu.CompilerParams(vmem_limit_bytes=(FRESH_LIMIT if any(fresh) else HELD_LIMIT) * MIB),
        cost_estimate=cost(4 * rows * depth * width, 4 * depth * width),
    )(base, x, *([sumsq] if summed else []), *weights)


def arrived_sum(keep, width, refs):
    total = keep[..., :width]
    for ref in refs:
        total = total + expand(ref, (slice(None), slice(None), slice(0, width)))
    if keep.shape[-1] == width:
        return total, None
    square = keep[..., width:]
    for ref in refs:
        square = square + jnp.sum(ref[:, :, width:].astype(F32), axis=-1, keepdims=True)
    return total, square


def add_kernel(count, width, pair, keep_ref, *refs):
    arrived, outs = refs[:count], refs[count:]
    total, square = arrived_sum(keep_ref[...], width, arrived)
    group = outs[0].shape[0]
    for i, out in enumerate(outs):
        rows = slice(None) if pair else slice(i * group, (i + 1) * group)
        out[:, :, :width] = total[rows] if i == 0 else squeeze(total[rows])
        if square is not None:
            out[:, :, width:] = square[rows] if i == 0 else three_lanes(square[rows][..., :1])


def add_stage(keep, width, arrived, size, pair):
    shape = (keep.shape[0] if pair else keep.shape[0] // size,) + keep.shape[1:]
    return pl.pallas_call(
        functools.partial(add_kernel, len(arrived), width, pair),
        out_shape=(struct(shape, F32),) + (struct(shape, BF16),) * (size - 1),
        in_specs=[VMEM] * (1 + len(arrived)),
        out_specs=(VMEM,) * size,
        name="add_partials",
        compiler_params=pltpu.CompilerParams(vmem_limit_bytes=8 * MIB),
        cost_estimate=cost(keep.size * 2, keep.size * 10),
    )(keep, *arrived)


def hidden_kernel(count, width, summed, features, pair, keep_ref, *refs):
    arrived, refs = refs[:count], refs[count:]
    out_ref = refs[0] if summed else refs[1]
    group = keep_ref.shape[0]
    per = keep_ref.shape[1] // 2
    made = []
    for p in range(group):
        total, square = arrived_sum(keep_ref[p : p + 1], width, [ref.at[pl.ds(group - 1 - p, 1)] for ref in arrived])
        total = total[0]
        rows = slice(p * per, (p + 1) * per)
        if summed:
            scale = 1.0 / jnp.sqrt(square[0][:per] / features + 1e-05)
            refs[1][rows] = scale
        else:
            scale = refs[0][rows]
        scale = scale[:, :1]
        gate, up = total[:per] * scale, total[per:] * scale
        made.append(gate / (1.0 + jnp.exp(-gate)) * up)
    out_ref[...] = jnp.concatenate(made, axis=0).astype(BF16)


def hidden_of(keep, width, arrived, scale, features, pair):
    group, both, _ = keep.shape
    rows = group * both // 2
    summed = scale is None
    out = struct((rows, width), BF16)
    return pl.pallas_call(
        functools.partial(hidden_kernel, len(arrived), width, summed, features, pair),
        out_shape=(out, struct((rows, LANES), F32)) if summed else (out,),
        in_specs=[VMEM] * (1 + len(arrived) + (not summed)),
        out_specs=(VMEM,) * (1 + summed),
        name="hidden",
        compiler_params=pltpu.CompilerParams(vmem_limit_bytes=8 * MIB),
        cost_estimate=cost(keep.size * 10, keep.size * 10),
    )(keep, *arrived, *([] if summed else [scale]))


def join_kernel(*refs):
    sources, out_ref = refs[:-1], refs[-1]
    out_ref[...] = jnp.concatenate([ref[...].astype(F32) for ref in sources], axis=0).astype(BF16)


def join(parts):
    rows, width = parts[0].shape
    return pl.pallas_call(
        join_kernel,
        out_shape=struct((rows * len(parts), width), BF16),
        in_specs=[VMEM] * len(parts),
        out_specs=VMEM,
        name="join",
        compiler_params=pltpu.CompilerParams(vmem_limit_bytes=8 * MIB),
        cost_estimate=cost(0, rows * len(parts) * width * 4),
    )(*parts)


def load_down_kernel(first, base_ref, down_hbm, after_ref, held, sems):
    row = pl.multiple_of(base_ref[0] + first, LANES)
    cuts = cuts_of(held.shape[0], 2 * PIECE)
    pairs = [(down_hbm.at[pl.ds(row + a, b - a), :], held.at[pl.ds(a, b - a), :]) for a, b in cuts]
    for copy in start_copies(pairs, sems):
        copy.wait()


def load_down(first, depth, base, weight, after):
    return pl.pallas_call(
        functools.partial(load_down_kernel, first),
        out_shape=struct((depth, weight.shape[1]), BF16),
        in_specs=[SMEM, HBM, VMEM],
        out_specs=VMEM,
        scratch_shapes=[pltpu.SemaphoreType.DMA((len(cuts_of(depth, 2 * PIECE)),))],
        name="load_down",
        compiler_params=pltpu.CompilerParams(vmem_limit_bytes=LOAD_LIMIT * MIB),
        cost_estimate=cost(0, 2 * depth * weight.shape[1]),
    )(base, weight, after)


def down_kernel(first, count, added, fresh, sent, base_ref, *refs):
    refs = list(refs)
    parts, weight, refs = refs[:count], refs[count], refs[count + 1 :]
    before = refs.pop(0) if added else None
    out_ref = refs.pop(0)
    send_ref = refs.pop(0) if sent else None
    if fresh:
        held, sems = refs
        row = pl.multiple_of(base_ref[0] + first, LANES)
        cuts = cuts_of(held.shape[0], 2 * PIECE)
        copies = start_copies([(weight.at[pl.ds(row + a, b - a), :], held.at[pl.ds(a, b - a), :]) for a, b in cuts], sems)
    else:
        held, cuts = weight, [(0, weight.shape[0])]
    hidden = jnp.concatenate([ref[...] for ref in parts], axis=0)
    total = before[...] if added else None
    for i, (a, b) in enumerate(cuts):
        if fresh:
            copies[i].wait()
        term = jnp.dot(hidden[:, a:b], held[a:b, :], preferred_element_type=F32)
        total = term if total is None else total + term
    out_ref[...] = total
    if sent:
        send_ref[...] = squeeze(total)


def down(first, base, parts, weight, before, fresh, sent):
    rows, width = sum(part.shape[0] for part in parts), weight.shape[1]
    depth = parts[0].shape[1]
    added = before is not None
    return pl.pallas_call(
        functools.partial(down_kernel, first, len(parts), added, fresh, sent),
        out_shape=(struct((rows, width), F32),)
        + (struct((rows, width), BF16),) * sent
        + (struct((depth, width), BF16),) * fresh,
        in_specs=[SMEM] + [VMEM] * len(parts) + [HBM if fresh else VMEM] + [VMEM] * added,
        out_specs=(VMEM,) * (1 + sent + fresh),
        scratch_shapes=[pltpu.SemaphoreType.DMA((len(cuts_of(depth, 2 * PIECE)),))] * fresh,
        name="down",
        compiler_params=pltpu.CompilerParams(vmem_limit_bytes=(DOWN_LIMIT if fresh else HELD_LIMIT) * MIB),
        cost_estimate=cost(2 * rows * depth * width, 2 * depth * width),
    )(base, *parts, weight, *([before] if added else []))


def chip_kernel(a_ref, b_ref, state_ref, state_out, send_ref):
    total = a_ref[...] + expand(b_ref)
    send_ref[...] = squeeze(total)
    state_out[...] = state_ref[...] + total


def renew_kernel(state_ref, *refs):
    arrived, (state_out, x_ref, sumsq_ref) = refs[:-3], refs[-3:]
    state = state_ref[...]
    for ref in arrived:
        state = state + expand(ref)
    state_out[...] = state
    x_ref[...] = state.astype(BF16)
    sumsq_ref[...] = rows_mean_square(state)


def finish_kernel(offsets, per, groups, where_ref, a_ref, b_ref, state_ref, out_ref, *refs):
    sends, (change, state) = refs[: groups - 1], refs[groups - 1 :]
    me, group = where_ref[0], where_ref[1]
    other = expand(b_ref)
    for p, offset in enumerate(offsets):
        first = (me ^ offset) * per
        if per % 8 == 0:
            first = pl.multiple_of(first, 8)
        rows = slice(p * per, (p + 1) * per)
        change[pl.ds(first, per), :] = a_ref[rows, :] + other[rows, :]
        state[pl.ds(first, per), :] = state_ref[rows, :]
    rows = out_ref.shape[0]
    own = pl.ds(pl.multiple_of(group * rows, 8), rows)
    out_ref[...] = state[own, :] + change[own, :]
    for k, ref in enumerate(sends):
        other = pl.multiple_of(lax.rem(group + k + 1, groups) * rows, 8)
        ref[...] = squeeze(change[pl.ds(other, rows), :])


def per_device(counts, tokens, gate_weight, up_weight, down_weight):
    groups, wide, ffn = counts
    stages, gathers = stages_of(wide, SCATTER_BITS), stages_of(wide, GATHER_BITS)
    offsets = [reverse(p, wide.bit_length() - 1) for p in range(wide)]
    rows = tokens.shape[0] * groups
    per = rows // wide
    features = tokens.shape[1] * wide
    share = gate_weight.shape[1] // groups
    edges = [share // LANES * sum(CHUNKS[:k]) // sum(CHUNKS) * LANES for k in range(len(CHUNKS) + 1)]
    chunks = [(a, b - a) for a, b in zip(edges, edges[1:])]
    me, group = lax.axis_index("wide"), lax.axis_index("groups")
    where = jnp.stack([me, group]).astype(jnp.int32)
    base = (group * share).astype(jnp.int32).reshape(1)

    def from_group(value, k):
        return lax.ppermute(value, "groups", [((i + k) % groups, i) for i in range(groups)])

    others = [from_group(tokens, k) for k in range(1, groups)]
    state, x, sumsq = arrange(offsets, per, groups, where, tokens, others)

    def scatter_stage(flips, sends):
        return [swap(send, "wide", flip, wide) for flip, send in zip(flips[1:], sends)]

    gate_weight, up_weight, down_weight = (in_hbm(w) for w in (gate_weight, up_weight, down_weight))
    last = len(chunks) - 1
    gates, downs = {}, {}
    early = load(*chunks[0], base, gate_weight)
    for step in range(STEPS):
        work, previous = [], x
        for c, (first, width) in enumerate(chunks):
            weights, fresh = gates.get(c, (gate_weight, up_weight)), (c not in gates,) * 2
            if fresh[0] and c == 0:
                weights, fresh = (early, up_weight), (False, True)
            size = len(stages[0])
            found = gate_up(
                first, width, per, size, base, after(x, previous), sumsq if c == 0 else None, weights, fresh
            )
            previous = found[0]
            if c not in gates:
                gates[c] = tuple(found[size:]) if c else (early, found[size])
            sends = list(found[1:size])
            if TIE and work:
                sends = [after(send, work[-1][1][0]) for send in sends]
            work.append((found[0], scatter_stage(stages[0], sends)))
        for at, flips in enumerate(stages[1:], 1):
            pair = PAIR and at + 1 == len(stages) and len(flips) == 2
            done = []
            for c, (first, width) in enumerate(chunks):
                keep, arrived = work[c]
                if c < last:
                    keep = after(keep, work[c + 1][0])
                elif c - 1 in downs and PRELOAD and step == 0:
                    keep = after(keep, downs[c - 1])
                keep, *sends = add_stage(keep, width, arrived, len(flips), pair)
                done.append((keep, scatter_stage(flips, sends)))
                if PRELOAD and c not in downs:
                    downs[c] = load_down(first, width, base, down_weight, keep)
            work = done
        scale, parts = None, []
        for c, (first, width) in enumerate(chunks):
            keep, arrived = work[c]
            if c < last:
                keep = after(keep, work[c + 1][0])
            elif c in downs:
                keep = after(keep, downs[c])
            made = hidden_of(keep, width, arrived, scale, features, pair)
            scale = made[1] if scale is None else scale
            parts.append([made[0]])
        for flips in reversed(gathers[:-1] if pair else gathers):
            done = []
            for c in range(len(chunks)):
                pieces = parts[c]
                if c < last and len(pieces) > 1:
                    pieces = [after(pieces[0], parts[c + 1][0])] + pieces[1:]
                done.append(pieces[0] if len(pieces) == 1 else join(pieces))
            for c in range(len(chunks)):
                whole = done[c]
                parts[c] = [whole] + [swap(whole, "wide", flip, wide) for flip in flips[1:]]
        change = None
        for c, (first, width) in enumerate(chunks):
            fresh = c not in downs
            if c < last:
                parts[c][0] = after(parts[c][0], parts[c + 1][0])
            found = down(first, base, parts[c], down_weight if fresh else downs[c], change, fresh, c == last)
            change = found[0]
            if fresh:
                downs[c] = found[-1]
        other = swap(found[1], "ffn", 1, ffn)
        if step + 1 < STEPS:
            shape = state.shape
            state, send = pl.pallas_call(
                chip_kernel,
                out_shape=(struct(shape, F32), struct(shape, BF16)),
                in_specs=[VMEM] * 3,
                out_specs=(VMEM,) * 2,
                name="chip_sum",
                compiler_params=pltpu.CompilerParams(vmem_limit_bytes=8 * MIB),
                cost_estimate=cost(state.size, state.size * 16),
            )(change, other, state)
            arrived = [from_group(send, k) for k in range(1, groups)]
            state, x, sumsq = pl.pallas_call(
                renew_kernel,
                out_shape=(struct(shape, F32), struct(shape, BF16), struct((rows, LANES), F32)),
                in_specs=[VMEM] * (1 + len(arrived)),
                out_specs=(VMEM,) * 3,
                name="renew",
                compiler_params=pltpu.CompilerParams(vmem_limit_bytes=8 * MIB),
                cost_estimate=cost(state.size, state.size * 12),
            )(state, *arrived)
    own = struct(tokens.shape, F32)
    out, *sends = pl.pallas_call(
        functools.partial(finish_kernel, offsets, per, groups),
        out_shape=(own,) + (struct(tokens.shape, BF16),) * (groups - 1),
        in_specs=[SMEM] + [VMEM] * 3,
        out_specs=(VMEM,) * groups,
        scratch_shapes=[pltpu.VMEM(state.shape, F32)] * 2,
        name="finish",
        compiler_params=pltpu.CompilerParams(vmem_limit_bytes=8 * MIB),
        cost_estimate=cost(state.size, state.size * 16),
    )(where, change, other, state)
    for k, send in enumerate(sends):
        arrived = from_group(send, groups - 1 - k)
        out = out + expand(arrived)
    return out


def solution(mesh):
    counts = tuple(mesh.shape[axis] for axis in ("groups", "wide", "ffn"))
    return jax.shard_map(
        functools.partial(per_device, counts),
        mesh=mesh,
        in_specs=(P("groups", "wide"), P("wide", "ffn"), P("wide", "ffn"), P("ffn", "wide")),
        out_specs=P("groups", "wide"),
        check_vma=False,
    )
```

```python
import functools

import jax
import jax.numpy as jnp
from jax import lax
from jax.experimental import pallas as pl
from jax.experimental.pallas import tpu as pltpu
from jax.sharding import PartitionSpec as P

STEPS = 2
CHUNKS = (27, 25)
SCATTER_BITS, GATHER_BITS = 2, 2
PRELOAD = True
TIE, PAIR = False, True
LANES = 128
PIECE = 256
F32 = jnp.float32
BF16 = jnp.bfloat16
SMEM = pl.BlockSpec(memory_space=pltpu.SMEM)
VMEM = pl.BlockSpec(memory_space=pltpu.VMEM)
HBM = pl.BlockSpec(memory_space=pltpu.HBM)
MIB = 2**20
LOAD_LIMIT, FRESH_LIMIT, DOWN_LIMIT, HELD_LIMIT = 10, 10, 10, 10


def struct(shape, dtype):
    return jax.ShapeDtypeStruct(shape, dtype)


def in_hbm(value):
    return pltpu.with_memory_space_constraint(value, pltpu.HBM)


def after(value, *earlier):
    return lax.optimization_barrier((value,) + earlier)[0]


def cost(flops, moved):
    return pl.CostEstimate(flops=int(flops), bytes_accessed=int(moved), transcendentals=0)


def stages_of(wide, most):
    found, low, total = [], 0, wide.bit_length() - 1
    while low < total:
        bits = min(most, total - low)
        found.append([reverse(i, bits) << low for i in range(1 << bits)])
        low += bits
    return found


def reverse(value, bits):
    return sum(((value >> k) & 1) << (bits - 1 - k) for k in range(bits))


def swap(value, axis, flip, count):
    return lax.ppermute(value, axis, [(i, i ^ flip) for i in range(count)])


def cuts_of(extent, piece):
    return [(a, min(a + piece, extent)) for a in range(0, extent, piece)]


def rows_mean_square(rows):
    total = jnp.sum(rows * rows, axis=1, keepdims=True)
    return jnp.broadcast_to(total, (rows.shape[0], LANES))


def arrange_kernel(offsets, per, groups, where_ref, own_ref, *refs):
    others, (state_ref, x_ref, sumsq_ref, whole) = refs[: groups - 1], refs[groups - 1 :]
    me, group = where_ref[0], where_ref[1]
    rows = own_ref.shape[0]
    for k, ref in enumerate((own_ref,) + tuple(others)):
        start = lax.rem(group + k, groups) * rows
        whole[pl.ds(pl.multiple_of(start, 8), rows), :] = ref[...].astype(F32)
    for p, offset in enumerate(offsets):
        first = (me ^ offset) * per
        if per % 8 == 0:
            first = pl.multiple_of(first, 8)
        state_ref[p * per : (p + 1) * per, :] = whole[pl.ds(first, per), :]
    state = state_ref[...]
    x_ref[...] = state.astype(BF16)
    sumsq_ref[...] = rows_mean_square(state)


def arrange(offsets, per, groups, where, own, others):
    rows, width = own.shape
    rows *= groups
    return pl.pallas_call(
        functools.partial(arrange_kernel, offsets, per, groups),
        out_shape=(struct((rows, width), F32), struct((rows, width), BF16), struct((rows, LANES), F32)),
        in_specs=[SMEM] + [VMEM] * groups,
        out_specs=(VMEM,) * 3,
        scratch_shapes=[pltpu.VMEM((rows, width), F32)],
        name="arrange",
        compiler_params=pltpu.CompilerParams(vmem_limit_bytes=8 * MIB),
        cost_estimate=cost(rows * width, rows * width * 10),
    )(where, own, *others)


def squeeze(value):
    return (value * jnp.abs(value)).astype(BF16)


def expand(ref, index=slice(None)):
    sent = ref[index].astype(F32)
    return sent * lax.rsqrt(jnp.maximum(jnp.abs(sent), 1e-37))


def three_lanes(value):
    shape = value.shape[:-1] + (LANES,)
    value = jnp.broadcast_to(value, shape)
    lane = lax.broadcasted_iota(jnp.int32, shape, len(shape) - 1)
    out = jnp.zeros(shape, F32)
    for k in range(3):
        part = value.astype(BF16).astype(F32)
        out = jnp.where(lane == k, part, out)
        value = value - part
    return out.astype(BF16)


def start_copies(pairs, sems):
    copies = [pltpu.make_async_copy(source, target, sems.at[i]) for i, (source, target) in enumerate(pairs)]
    for copy in copies:
        copy.start()
    return copies


def column_pairs(column, width, sources, targets):
    pairs = []
    for a, b in cuts_of(targets[0].shape[0], PIECE):
        for source, target in zip(sources, targets):
            pairs.append((source.at[pl.ds(a, b - a), pl.ds(column, width)], target.at[pl.ds(a, b - a), :]))
    return pairs


def load_kernel(first, base_ref, weight_hbm, held_ref, sems):
    column = pl.multiple_of(base_ref[0] + first, LANES)
    for copy in start_copies(column_pairs(column, held_ref.shape[1], (weight_hbm,), (held_ref,)), sems):
        copy.wait()


def load(first, width, base, weight):
    depth = weight.shape[0]
    return pl.pallas_call(
        functools.partial(load_kernel, first),
        out_shape=struct((depth, width), BF16),
        in_specs=[SMEM, HBM],
        out_specs=VMEM,
        scratch_shapes=[pltpu.SemaphoreType.DMA((len(cuts_of(depth, PIECE)),))],
        name="load",
        compiler_params=pltpu.CompilerParams(vmem_limit_bytes=LOAD_LIMIT * MIB),
        cost_estimate=cost(0, 4 * depth * width),
    )(base, weight)


def gate_up_kernel(first, per, size, fresh, summed, base_ref, x_ref, *refs):
    refs = list(refs)
    sumsq_ref = refs.pop(0) if summed else None
    weights, refs = refs[:2], refs[2:]
    outs, refs = refs[:size], refs[size:]
    column = pl.multiple_of(base_ref[0] + first, LANES)
    held, copies = [], []
    for k in range(2):
        target = refs.pop(0) if fresh[k] else weights[k]
        held.append(target)
        copies.append((weights[k], target) if fresh[k] else None)
    depth, width = held[0].shape
    cuts = cuts_of(depth, PIECE)
    for k in range(2):
        if fresh[k]:
            sems = refs.pop(0)
            copies[k] = start_copies(column_pairs(column, width, copies[k][:1], copies[k][1:]), sems)
    totals = [None, None]
    order = [(i, k) for i in range(len(cuts)) for k in range(2)]
    if fresh[0] != fresh[1]:
        order.sort(key=lambda one: fresh[one[1]])
    for i, k in order:
        a, b = cuts[i]
        if fresh[k]:
            copies[k][i].wait()
        term = jnp.dot(x_ref[:, a:b], held[k][a:b, :], preferred_element_type=F32)
        totals[k] = term if totals[k] is None else totals[k] + term
    hand_out(totals, outs, width, per, sumsq_ref[...] if summed else None)


def hand_out(totals, outs, width, per, squares):
    size, group = len(outs), outs[0].shape[0]
    for p in range(group * size):
        rows = slice(p * per, (p + 1) * per)
        both = jnp.concatenate([totals[0][rows], totals[1][rows]], axis=0)
        target = outs[p // group]
        target[p % group, :, :width] = both if p < group else squeeze(both)
        if squares is not None:
            square = jnp.concatenate([squares[rows], squares[rows]], axis=0)
            target[p % group, :, width:] = square if p < group else three_lanes(square[:, :1])


def renewed(state_ref, arrived):
    state = state_ref[...]
    for ref in arrived:
        state = state + expand(ref)
    return state


def begin_kernel(count, state_ref, *refs):
    arrived, (gate_ref, up_ref, state_out, x_ref, sumsq_ref, gate_out, up_out) = refs[:count], refs[count:]
    state = renewed(state_ref, arrived)
    half = state.shape[1]
    x = state.astype(BF16)
    state_out[...] = state
    x_ref[...] = x
    sumsq_ref[...] = rows_mean_square(state)
    gate_out[...] = jnp.dot(x, gate_ref[:half, :], preferred_element_type=F32)
    up_out[...] = jnp.dot(x, up_ref[:half, :], preferred_element_type=F32)


def end_kernel(count, per, size, state_ref, *refs):
    arrived, refs = refs[:count], refs[count:]
    gate_ref, up_ref, first_state, first_x, sumsq_ref, gate_in, up_in, *outs = refs
    outs, (state_out, x_ref) = outs[:size], outs[size:]
    state = renewed(state_ref, arrived)
    half, width = state.shape[1], gate_ref.shape[1]
    x = state.astype(BF16)
    state_out[:, :half] = first_state[...]
    state_out[:, half:] = state
    x_ref[:, :half] = first_x[...]
    x_ref[:, half:] = x
    totals = [gate_in[...] + jnp.dot(x, gate_ref[half:, :], preferred_element_type=F32)]
    totals.append(up_in[...] + jnp.dot(x, up_ref[half:, :], preferred_element_type=F32))
    hand_out(totals, outs, width, per, sumsq_ref[...] + rows_mean_square(state))


def renew_and_gate_up(per, size, states, sends, weights):
    rows, half = states[0].shape
    depth, width = weights[0].shape
    params = dict(compiler_params=pltpu.CompilerParams(vmem_limit_bytes=HELD_LIMIT * MIB))
    params["cost_estimate"] = cost(2 * rows * depth * width, 2 * depth * width)
    total = struct((rows, width), F32)
    made = pl.pallas_call(
        functools.partial(begin_kernel, len(sends[0])),
        out_shape=(struct((rows, half), F32), struct((rows, half), BF16), struct((rows, LANES), F32), total, total),
        in_specs=[VMEM] * (3 + len(sends[0])),
        out_specs=(VMEM,) * 5,
        name="begin",
        **params,
    )(states[0], *sends[0], *weights)
    shape = (rows // per // size, 2 * per, width + LANES)
    return pl.pallas_call(
        functools.partial(end_kernel, len(sends[1]), per, size),
        out_shape=(struct(shape, F32),)
        + (struct(shape, BF16),) * (size - 1)
        + (struct((rows, depth), F32), struct((rows, depth), BF16)),
        in_specs=[VMEM] * (8 + len(sends[1])),
        out_specs=(VMEM,) * (size + 2),
        name="end",
        **params,
    )(states[1], *sends[1], *weights, *made)


def gate_up(first, width, per, size, base, x, sumsq, weights, fresh):
    rows, depth = x.shape
    group = rows // per // size
    summed = sumsq is not None
    shape = (group, 2 * per, width + LANES * summed)
    held = struct((depth, width), BF16)
    return pl.pallas_call(
        functools.partial(gate_up_kernel, first, per, size, fresh, summed),
        out_shape=(struct(shape, F32),) + (struct(shape, BF16),) * (size - 1) + (held,) * sum(fresh),
        in_specs=[SMEM, VMEM] + [VMEM] * summed + [HBM if one else VMEM for one in fresh],
        out_specs=(VMEM,) * (size + sum(fresh)),
        scratch_shapes=[pltpu.SemaphoreType.DMA((len(cuts_of(depth, PIECE)),))] * sum(fresh),
        name="gate_up",
        compiler_params=pltpu.CompilerParams(vmem_limit_bytes=(FRESH_LIMIT if any(fresh) else HELD_LIMIT) * MIB),
        cost_estimate=cost(4 * rows * depth * width, 4 * depth * width),
    )(base, x, *([sumsq] if summed else []), *weights)


def arrived_sum(keep, width, refs):
    total = keep[..., :width]
    for ref in refs:
        total = total + expand(ref, (slice(None), slice(None), slice(0, width)))
    if keep.shape[-1] == width:
        return total, None
    square = keep[..., width:]
    for ref in refs:
        square = square + jnp.sum(ref[:, :, width:].astype(F32), axis=-1, keepdims=True)
    return total, square


def add_kernel(count, width, pair, keep_ref, *refs):
    arrived, outs = refs[:count], refs[count:]
    total, square = arrived_sum(keep_ref[...], width, arrived)
    group = outs[0].shape[0]
    for i, out in enumerate(outs):
        rows = slice(None) if pair else slice(i * group, (i + 1) * group)
        out[:, :, :width] = total[rows] if i == 0 else squeeze(total[rows])
        if square is not None:
            out[:, :, width:] = square[rows] if i == 0 else three_lanes(square[rows][..., :1])


def add_stage(keep, width, arrived, size, pair):
    shape = (keep.shape[0] if pair else keep.shape[0] // size,) + keep.shape[1:]
    return pl.pallas_call(
        functools.partial(add_kernel, len(arrived), width, pair),
        out_shape=(struct(shape, F32),) + (struct(shape, BF16),) * (size - 1),
        in_specs=[VMEM] * (1 + len(arrived)),
        out_specs=(VMEM,) * size,
        name="add_partials",
        compiler_params=pltpu.CompilerParams(vmem_limit_bytes=8 * MIB),
        cost_estimate=cost(keep.size * 2, keep.size * 10),
    )(keep, *arrived)


def hidden_kernel(count, width, summed, features, pair, keep_ref, *refs):
    arrived, refs = refs[:count], refs[count:]
    out_ref = refs[0] if summed else refs[1]
    group = keep_ref.shape[0]
    per = keep_ref.shape[1] // 2
    made = []
    for p in range(group):
        total, square = arrived_sum(keep_ref[p : p + 1], width, [ref.at[pl.ds(group - 1 - p, 1)] for ref in arrived])
        total = total[0]
        rows = slice(p * per, (p + 1) * per)
        if summed:
            scale = 1.0 / jnp.sqrt(square[0][:per] / features + 1e-05)
            refs[1][rows] = scale
        else:
            scale = refs[0][rows]
        scale = scale[:, :1]
        gate, up = total[:per] * scale, total[per:] * scale
        made.append(gate / (1.0 + jnp.exp(-gate)) * up)
    out_ref[...] = jnp.concatenate(made, axis=0).astype(BF16)


def hidden_of(keep, width, arrived, scale, features, pair):
    group, both, _ = keep.shape
    rows = group * both // 2
    summed = scale is None
    out = struct((rows, width), BF16)
    return pl.pallas_call(
        functools.partial(hidden_kernel, len(arrived), width, summed, features, pair),
        out_shape=(out, struct((rows, LANES), F32)) if summed else (out,),
        in_specs=[VMEM] * (1 + len(arrived) + (not summed)),
        out_specs=(VMEM,) * (1 + summed),
        name="hidden",
        compiler_params=pltpu.CompilerParams(vmem_limit_bytes=8 * MIB),
        cost_estimate=cost(keep.size * 10, keep.size * 10),
    )(keep, *arrived, *([] if summed else [scale]))


def join_kernel(*refs):
    sources, out_ref = refs[:-1], refs[-1]
    out_ref[...] = jnp.concatenate([ref[...].astype(F32) for ref in sources], axis=0).astype(BF16)


def join(parts):
    rows, width = parts[0].shape
    return pl.pallas_call(
        join_kernel,
        out_shape=struct((rows * len(parts), width), BF16),
        in_specs=[VMEM] * len(parts),
        out_specs=VMEM,
        name="join",
        compiler_params=pltpu.CompilerParams(vmem_limit_bytes=8 * MIB),
        cost_estimate=cost(0, rows * len(parts) * width * 4),
    )(*parts)


def load_down_kernel(first, base_ref, down_hbm, after_ref, held, sems):
    row = pl.multiple_of(base_ref[0] + first, LANES)
    cuts = cuts_of(held.shape[0], 2 * PIECE)
    pairs = [(down_hbm.at[pl.ds(row + a, b - a), :], held.at[pl.ds(a, b - a), :]) for a, b in cuts]
    for copy in start_copies(pairs, sems):
        copy.wait()


def load_down(first, depth, base, weight, after):
    return pl.pallas_call(
        functools.partial(load_down_kernel, first),
        out_shape=struct((depth, weight.shape[1]), BF16),
        in_specs=[SMEM, HBM, VMEM],
        out_specs=VMEM,
        scratch_shapes=[pltpu.SemaphoreType.DMA((len(cuts_of(depth, 2 * PIECE)),))],
        name="load_down",
        compiler_params=pltpu.CompilerParams(vmem_limit_bytes=LOAD_LIMIT * MIB),
        cost_estimate=cost(0, 2 * depth * weight.shape[1]),
    )(base, weight, after)


def down_kernel(first, count, added, fresh, sent, base_ref, *refs):
    refs = list(refs)
    parts, weight, refs = refs[:count], refs[count], refs[count + 1 :]
    before = refs.pop(0) if added else None
    out_ref = refs.pop(0)
    send_ref = refs.pop(0) if sent else None
    if fresh:
        held, sems = refs
        row = pl.multiple_of(base_ref[0] + first, LANES)
        cuts = cuts_of(held.shape[0], 2 * PIECE)
        copies = start_copies([(weight.at[pl.ds(row + a, b - a), :], held.at[pl.ds(a, b - a), :]) for a, b in cuts], sems)
    else:
        held, cuts = weight, [(0, weight.shape[0])]
    hidden = jnp.concatenate([ref[...] for ref in parts], axis=0)
    total = before[...] if added else None
    for i, (a, b) in enumerate(cuts):
        if fresh:
            copies[i].wait()
        term = jnp.dot(hidden[:, a:b], held[a:b, :], preferred_element_type=F32)
        total = term if total is None else total + term
    out_ref[...] = total
    if sent:
        send_ref[...] = squeeze(total)


def down(first, base, parts, weight, before, fresh, sent):
    rows, width = sum(part.shape[0] for part in parts), weight.shape[1]
    depth = parts[0].shape[1]
    added = before is not None
    return pl.pallas_call(
        functools.partial(down_kernel, first, len(parts), added, fresh, sent),
        out_shape=(struct((rows, width), F32),)
        + (struct((rows, width), BF16),) * sent
        + (struct((depth, width), BF16),) * fresh,
        in_specs=[SMEM] + [VMEM] * len(parts) + [HBM if fresh else VMEM] + [VMEM] * added,
        out_specs=(VMEM,) * (1 + sent + fresh),
        scratch_shapes=[pltpu.SemaphoreType.DMA((len(cuts_of(depth, 2 * PIECE)),))] * fresh,
        name="down",
        compiler_params=pltpu.CompilerParams(vmem_limit_bytes=(DOWN_LIMIT if fresh else HELD_LIMIT) * MIB),
        cost_estimate=cost(2 * rows * depth * width, 2 * depth * width),
    )(base, *parts, weight, *([before] if added else []))


def chip_kernel(a_ref, b_ref, state_ref, *outs):
    total = a_ref[...] + expand(b_ref)
    state = state_ref[...] + total
    half = outs[0].shape[1]
    for k in range(2):
        columns = slice(k * half, (k + 1) * half)
        outs[k][...] = state[:, columns]
        outs[2 + k][...] = squeeze(total[:, columns])


def finish_kernel(offsets, per, groups, where_ref, a_ref, b_ref, state_ref, out_ref, *refs):
    sends, (change, state) = refs[: groups - 1], refs[groups - 1 :]
    me, group = where_ref[0], where_ref[1]
    other = expand(b_ref)
    for p, offset in enumerate(offsets):
        first = (me ^ offset) * per
        if per % 8 == 0:
            first = pl.multiple_of(first, 8)
        rows = slice(p * per, (p + 1) * per)
        change[pl.ds(first, per), :] = a_ref[rows, :] + other[rows, :]
        state[pl.ds(first, per), :] = state_ref[rows, :]
    rows = out_ref.shape[0]
    own = pl.ds(pl.multiple_of(group * rows, 8), rows)
    out_ref[...] = state[own, :] + change[own, :]
    for k, ref in enumerate(sends):
        other = pl.multiple_of(lax.rem(group + k + 1, groups) * rows, 8)
        ref[...] = squeeze(change[pl.ds(other, rows), :])


def per_device(counts, tokens, gate_weight, up_weight, down_weight):
    groups, wide, ffn = counts
    stages, gathers = stages_of(wide, SCATTER_BITS), stages_of(wide, GATHER_BITS)
    offsets = [reverse(p, wide.bit_length() - 1) for p in range(wide)]
    rows = tokens.shape[0] * groups
    per = rows // wide
    features = tokens.shape[1] * wide
    share = gate_weight.shape[1] // groups
    edges = [share // LANES * sum(CHUNKS[:k]) // sum(CHUNKS) * LANES for k in range(len(CHUNKS) + 1)]
    chunks = [(a, b - a) for a, b in zip(edges, edges[1:])]
    me, group = lax.axis_index("wide"), lax.axis_index("groups")
    where = jnp.stack([me, group]).astype(jnp.int32)
    base = (group * share).astype(jnp.int32).reshape(1)

    def from_group(value, k):
        return lax.ppermute(value, "groups", [((i + k) % groups, i) for i in range(groups)])

    others = [from_group(tokens, k) for k in range(1, groups)]
    state, x, sumsq = arrange(offsets, per, groups, where, tokens, others)

    def scatter_stage(flips, sends):
        return [swap(send, "wide", flip, wide) for flip, send in zip(flips[1:], sends)]

    gate_weight, up_weight, down_weight = (in_hbm(w) for w in (gate_weight, up_weight, down_weight))
    last = len(chunks) - 1
    gates, downs = {}, {}
    early = load(*chunks[0], base, gate_weight)
    for step in range(STEPS):
        work, previous = [], x
        for c, (first, width) in enumerate(chunks):
            weights, fresh = gates.get(c, (gate_weight, up_weight)), (c not in gates,) * 2
            if fresh[0] and c == 0:
                weights, fresh = (early, up_weight), (False, True)
            size = len(stages[0])
            if step > 0 and c == 0:
                *found, state, x = renew_and_gate_up(per, size, states, halves, weights)
            else:
                found = gate_up(
                    first, width, per, size, base, after(x, previous), sumsq if c == 0 else None, weights, fresh
                )
            previous = found[0]
            if c not in gates:
                gates[c] = tuple(found[size:]) if c else (early, found[size])
            sends = list(found[1:size])
            if TIE and work:
                sends = [after(send, work[-1][1][0]) for send in sends]
            work.append((found[0], scatter_stage(stages[0], sends)))
        for at, flips in enumerate(stages[1:], 1):
            pair = PAIR and at + 1 == len(stages) and len(flips) == 2
            done = []
            for c, (first, width) in enumerate(chunks):
                keep, arrived = work[c]
                if c < last:
                    keep = after(keep, work[c + 1][0])
                elif c - 1 in downs and PRELOAD and step == 0:
                    keep = after(keep, downs[c - 1])
                keep, *sends = add_stage(keep, width, arrived, len(flips), pair)
                done.append((keep, scatter_stage(flips, sends)))
                if PRELOAD and c not in downs:
                    downs[c] = load_down(first, width, base, down_weight, keep)
            work = done
        scale, parts = None, []
        for c, (first, width) in enumerate(chunks):
            keep, arrived = work[c]
            if c < last:
                keep = after(keep, work[c + 1][0])
            elif c in downs:
                keep = after(keep, downs[c])
            made = hidden_of(keep, width, arrived, scale, features, pair)
            scale = made[1] if scale is None else scale
            parts.append([made[0]])
        for flips in reversed(gathers[:-1] if pair else gathers):
            done = []
            for c in range(len(chunks)):
                pieces = parts[c]
                if c < last and len(pieces) > 1:
                    pieces = [after(pieces[0], parts[c + 1][0])] + pieces[1:]
                done.append(pieces[0] if len(pieces) == 1 else join(pieces))
            for c in range(len(chunks)):
                whole = done[c]
                parts[c] = [whole] + [swap(whole, "wide", flip, wide) for flip in flips[1:]]
        change = None
        for c, (first, width) in enumerate(chunks):
            fresh = c not in downs
            if c < last:
                parts[c][0] = after(parts[c][0], parts[c + 1][0])
            found = down(first, base, parts[c], down_weight if fresh else downs[c], change, fresh, c == last)
            change = found[0]
            if fresh:
                downs[c] = found[-1]
        other = swap(found[1], "ffn", 1, ffn)
        if step + 1 < STEPS:
            half = struct((rows, state.shape[1] // 2), F32)
            sent = struct(half.shape, BF16)
            *states, first_send, second_send = pl.pallas_call(
                chip_kernel,
                out_shape=(half, half, sent, sent),
                in_specs=[VMEM] * 3,
                out_specs=(VMEM,) * 4,
                name="chip_sum",
                compiler_params=pltpu.CompilerParams(vmem_limit_bytes=8 * MIB),
                cost_estimate=cost(state.size, state.size * 16),
            )(change, other, state)
            halves = [[from_group(send, k) for k in range(1, groups)] for send in (first_send, second_send)]
    own = struct(tokens.shape, F32)
    out, *sends = pl.pallas_call(
        functools.partial(finish_kernel, offsets, per, groups),
        out_shape=(own,) + (struct(tokens.shape, BF16),) * (groups - 1),
        in_specs=[SMEM] + [VMEM] * 3,
        out_specs=(VMEM,) * groups,
        scratch_shapes=[pltpu.VMEM(state.shape, F32)] * 2,
        name="finish",
        compiler_params=pltpu.CompilerParams(vmem_limit_bytes=8 * MIB),
        cost_estimate=cost(state.size, state.size * 16),
    )(where, change, other, state)
    for k, send in enumerate(sends):
        arrived = from_group(send, groups - 1 - k)
        out = out + expand(arrived)
    return out


def solution(mesh):
    counts = tuple(mesh.shape[axis] for axis in ("groups", "wide", "ffn"))
    return jax.shard_map(
        functools.partial(per_device, counts),
        mesh=mesh,
        in_specs=(P("groups", "wide"), P("wide", "ffn"), P("wide", "ffn"), P("ffn", "wide")),
        out_specs=P("groups", "wide"),
        check_vma=False,
    )
```

```python
import functools

import jax
import jax.numpy as jnp
from jax import lax
from jax.experimental import pallas as pl
from jax.experimental.pallas import tpu as pltpu
from jax.sharding import PartitionSpec as P

STEPS = 2
CHUNKS = (27, 25)
SCATTER_BITS, GATHER_BITS = 2, 2
PRELOAD = True
TIE, PAIR = False, True
LANES = 128
PIECE = 256
F32 = jnp.float32
BF16 = jnp.bfloat16
SMEM = pl.BlockSpec(memory_space=pltpu.SMEM)
VMEM = pl.BlockSpec(memory_space=pltpu.VMEM)
HBM = pl.BlockSpec(memory_space=pltpu.HBM)
MIB = 2**20
LOAD_LIMIT, FRESH_LIMIT, DOWN_LIMIT, HELD_LIMIT = 10, 10, 10, 10


def struct(shape, dtype):
    return jax.ShapeDtypeStruct(shape, dtype)


def in_hbm(value):
    return pltpu.with_memory_space_constraint(value, pltpu.HBM)


def after(value, *earlier):
    return lax.optimization_barrier((value,) + earlier)[0]


def cost(flops, moved):
    return pl.CostEstimate(flops=int(flops), bytes_accessed=int(moved), transcendentals=0)


def stages_of(wide, most):
    found, low, total = [], 0, wide.bit_length() - 1
    while low < total:
        bits = min(most, total - low)
        found.append([reverse(i, bits) << low for i in range(1 << bits)])
        low += bits
    return found


def reverse(value, bits):
    return sum(((value >> k) & 1) << (bits - 1 - k) for k in range(bits))


def swap(value, axis, flip, count):
    return lax.ppermute(value, axis, [(i, i ^ flip) for i in range(count)])


def cuts_of(extent, piece):
    return [(a, min(a + piece, extent)) for a in range(0, extent, piece)]


def rows_mean_square(rows):
    total = jnp.sum(rows * rows, axis=1, keepdims=True)
    return jnp.broadcast_to(total, (rows.shape[0], LANES))


def arrange_kernel(offsets, per, groups, where_ref, own_ref, *refs):
    others, (state_ref, x_ref, sumsq_ref, whole) = refs[: groups - 1], refs[groups - 1 :]
    me, group = where_ref[0], where_ref[1]
    rows = own_ref.shape[0]
    for k, ref in enumerate((own_ref,) + tuple(others)):
        start = lax.rem(group + k, groups) * rows
        whole[pl.ds(pl.multiple_of(start, 8), rows), :] = ref[...].astype(F32)
    for p, offset in enumerate(offsets):
        first = (me ^ offset) * per
        if per % 8 == 0:
            first = pl.multiple_of(first, 8)
        state_ref[p * per : (p + 1) * per, :] = whole[pl.ds(first, per), :]
    state = state_ref[...]
    x_ref[...] = state.astype(BF16)
    sumsq_ref[...] = rows_mean_square(state)


def arrange(offsets, per, groups, where, own, others):
    rows, width = own.shape
    rows *= groups
    return pl.pallas_call(
        functools.partial(arrange_kernel, offsets, per, groups),
        out_shape=(struct((rows, width), F32), struct((rows, width), BF16), struct((rows, LANES), F32)),
        in_specs=[SMEM] + [VMEM] * groups,
        out_specs=(VMEM,) * 3,
        scratch_shapes=[pltpu.VMEM((rows, width), F32)],
        name="arrange",
        compiler_params=pltpu.CompilerParams(vmem_limit_bytes=8 * MIB),
        cost_estimate=cost(rows * width, rows * width * 10),
    )(where, own, *others)


def squeeze(value):
    return (value * jnp.abs(value)).astype(BF16)


def expand(ref, index=slice(None)):
    sent = ref[index].astype(F32)
    return sent * lax.rsqrt(jnp.maximum(jnp.abs(sent), 1e-37))


def three_lanes(value):
    shape = value.shape[:-1] + (LANES,)
    value = jnp.broadcast_to(value, shape)
    lane = lax.broadcasted_iota(jnp.int32, shape, len(shape) - 1)
    out = jnp.zeros(shape, F32)
    for k in range(3):
        part = value.astype(BF16).astype(F32)
        out = jnp.where(lane == k, part, out)
        value = value - part
    return out.astype(BF16)


def start_copies(pairs, sems):
    copies = [pltpu.make_async_copy(source, target, sems.at[i]) for i, (source, target) in enumerate(pairs)]
    for copy in copies:
        copy.start()
    return copies


def column_pairs(column, width, sources, targets):
    pairs = []
    for a, b in cuts_of(targets[0].shape[0], PIECE):
        for source, target in zip(sources, targets):
            pairs.append((source.at[pl.ds(a, b - a), pl.ds(column, width)], target.at[pl.ds(a, b - a), :]))
    return pairs


def load_kernel(first, base_ref, weight_hbm, held_ref, sems):
    column = pl.multiple_of(base_ref[0] + first, LANES)
    for copy in start_copies(column_pairs(column, held_ref.shape[1], (weight_hbm,), (held_ref,)), sems):
        copy.wait()


def load(first, width, base, weight):
    depth = weight.shape[0]
    return pl.pallas_call(
        functools.partial(load_kernel, first),
        out_shape=struct((depth, width), BF16),
        in_specs=[SMEM, HBM],
        out_specs=VMEM,
        scratch_shapes=[pltpu.SemaphoreType.DMA((len(cuts_of(depth, PIECE)),))],
        name="load",
        compiler_params=pltpu.CompilerParams(vmem_limit_bytes=LOAD_LIMIT * MIB),
        cost_estimate=cost(0, 4 * depth * width),
    )(base, weight)


def gate_up_kernel(first, per, size, fresh, summed, base_ref, x_ref, *refs):
    refs = list(refs)
    sumsq_ref = refs.pop(0) if summed else None
    weights, refs = refs[:2], refs[2:]
    outs, refs = refs[:size], refs[size:]
    column = pl.multiple_of(base_ref[0] + first, LANES)
    held, copies = [], []
    for k in range(2):
        target = refs.pop(0) if fresh[k] else weights[k]
        held.append(target)
        copies.append((weights[k], target) if fresh[k] else None)
    depth, width = held[0].shape
    cuts = cuts_of(depth, PIECE)
    for k in range(2):
        if fresh[k]:
            sems = refs.pop(0)
            copies[k] = start_copies(column_pairs(column, width, copies[k][:1], copies[k][1:]), sems)
    totals = [None, None]
    order = [(i, k) for i in range(len(cuts)) for k in range(2)]
    if fresh[0] != fresh[1]:
        order.sort(key=lambda one: fresh[one[1]])
    for i, k in order:
        a, b = cuts[i]
        if fresh[k]:
            copies[k][i].wait()
        term = jnp.dot(x_ref[:, a:b], held[k][a:b, :], preferred_element_type=F32)
        totals[k] = term if totals[k] is None else totals[k] + term
    hand_out(totals, outs, width, per, sumsq_ref[...] if summed else None)


def hand_out(totals, outs, width, per, squares):
    size, group = len(outs), outs[0].shape[0]
    for p in range(group * size):
        rows = slice(p * per, (p + 1) * per)
        both = jnp.concatenate([totals[0][rows], totals[1][rows]], axis=0)
        target = outs[p // group]
        target[p % group, :, :width] = both if p < group else squeeze(both)
        if squares is not None:
            square = jnp.concatenate([squares[rows], squares[rows]], axis=0)
            target[p % group, :, width:] = square if p < group else three_lanes(square[:, :1])


def renewed(state_ref, arrived):
    state = state_ref[...]
    for ref in arrived:
        state = state + expand(ref)
    return state


def begin_kernel(count, state_ref, *refs):
    arrived, (gate_ref, up_ref, state_out, x_ref, sumsq_ref, gate_out, up_out) = refs[:count], refs[count:]
    state = renewed(state_ref, arrived)
    half = state.shape[1]
    x = state.astype(BF16)
    state_out[...] = state
    x_ref[...] = x
    sumsq_ref[...] = rows_mean_square(state)
    gate_out[...] = jnp.dot(x, gate_ref[:half, :], preferred_element_type=F32)
    up_out[...] = jnp.dot(x, up_ref[:half, :], preferred_element_type=F32)


def end_kernel(count, per, size, state_ref, *refs):
    arrived, refs = refs[:count], refs[count:]
    gate_ref, up_ref, first_state, first_x, sumsq_ref, gate_in, up_in, *outs = refs
    outs, (state_out, x_ref) = outs[:size], outs[size:]
    state = renewed(state_ref, arrived)
    half, width = state.shape[1], gate_ref.shape[1]
    x = state.astype(BF16)
    state_out[:, :half] = first_state[...]
    state_out[:, half:] = state
    x_ref[:, :half] = first_x[...]
    x_ref[:, half:] = x
    totals = [gate_in[...] + jnp.dot(x, gate_ref[half:, :], preferred_element_type=F32)]
    totals.append(up_in[...] + jnp.dot(x, up_ref[half:, :], preferred_element_type=F32))
    hand_out(totals, outs, width, per, sumsq_ref[...] + rows_mean_square(state))


def renew_and_gate_up(per, size, states, sends, weights):
    rows, half = states[0].shape
    depth, width = weights[0].shape
    params = dict(compiler_params=pltpu.CompilerParams(vmem_limit_bytes=HELD_LIMIT * MIB))
    params["cost_estimate"] = cost(2 * rows * depth * width, 2 * depth * width)
    total = struct((rows, width), F32)
    made = pl.pallas_call(
        functools.partial(begin_kernel, len(sends[0])),
        out_shape=(struct((rows, half), F32), struct((rows, half), BF16), struct((rows, LANES), F32), total, total),
        in_specs=[VMEM] * (3 + len(sends[0])),
        out_specs=(VMEM,) * 5,
        name="begin",
        **params,
    )(states[0], *sends[0], *weights)
    shape = (rows // per // size, 2 * per, width + LANES)
    return pl.pallas_call(
        functools.partial(end_kernel, len(sends[1]), per, size),
        out_shape=(struct(shape, F32),)
        + (struct(shape, BF16),) * (size - 1)
        + (struct((rows, depth), F32), struct((rows, depth), BF16)),
        in_specs=[VMEM] * (8 + len(sends[1])),
        out_specs=(VMEM,) * (size + 2),
        name="end",
        **params,
    )(states[1], *sends[1], *weights, *made)


def gate_up(first, width, per, size, base, x, sumsq, weights, fresh):
    rows, depth = x.shape
    group = rows // per // size
    summed = sumsq is not None
    shape = (group, 2 * per, width + LANES * summed)
    held = struct((depth, width), BF16)
    return pl.pallas_call(
        functools.partial(gate_up_kernel, first, per, size, fresh, summed),
        out_shape=(struct(shape, F32),) + (struct(shape, BF16),) * (size - 1) + (held,) * sum(fresh),
        in_specs=[SMEM, VMEM] + [VMEM] * summed + [HBM if one else VMEM for one in fresh],
        out_specs=(VMEM,) * (size + sum(fresh)),
        scratch_shapes=[pltpu.SemaphoreType.DMA((len(cuts_of(depth, PIECE)),))] * sum(fresh),
        name="gate_up",
        compiler_params=pltpu.CompilerParams(vmem_limit_bytes=(FRESH_LIMIT if any(fresh) else HELD_LIMIT) * MIB),
        cost_estimate=cost(4 * rows * depth * width, 4 * depth * width),
    )(base, x, *([sumsq] if summed else []), *weights)


def arrived_sum(keep, width, refs):
    total = keep[..., :width]
    for ref in refs:
        total = total + expand(ref, (slice(None), slice(None), slice(0, width)))
    if keep.shape[-1] == width:
        return total, None
    square = keep[..., width:]
    lanes = sum(ref[:, :, width:].astype(F32) for ref in refs)
    return total, square + jnp.sum(lanes, axis=-1, keepdims=True)


def add_kernel(count, width, pair, keep_ref, *refs):
    arrived, outs = refs[:count], refs[count:]
    total, square = arrived_sum(keep_ref[...], width, arrived)
    group = outs[0].shape[0]
    for i, out in enumerate(outs):
        rows = slice(None) if pair else slice(i * group, (i + 1) * group)
        out[:, :, :width] = total[rows] if i == 0 else squeeze(total[rows])
        if square is not None:
            out[:, :, width:] = square[rows] if i == 0 else three_lanes(square[rows][..., :1])


def add_stage(keep, width, arrived, size, pair):
    shape = (keep.shape[0] if pair else keep.shape[0] // size,) + keep.shape[1:]
    return pl.pallas_call(
        functools.partial(add_kernel, len(arrived), width, pair),
        out_shape=(struct(shape, F32),) + (struct(shape, BF16),) * (size - 1),
        in_specs=[VMEM] * (1 + len(arrived)),
        out_specs=(VMEM,) * size,
        name="add_partials",
        compiler_params=pltpu.CompilerParams(vmem_limit_bytes=8 * MIB),
        cost_estimate=cost(keep.size * 2, keep.size * 10),
    )(keep, *arrived)


def hidden_kernel(count, width, summed, features, pair, keep_ref, *refs):
    arrived, refs = refs[:count], refs[count:]
    out_ref = refs[0] if summed else refs[1]
    group = keep_ref.shape[0]
    per = keep_ref.shape[1] // 2
    made = []
    for p in range(group):
        total, square = arrived_sum(keep_ref[p : p + 1], width, [ref.at[pl.ds(group - 1 - p, 1)] for ref in arrived])
        total = total[0]
        rows = slice(p * per, (p + 1) * per)
        if summed:
            scale = 1.0 / jnp.sqrt(square[0][:per] / features + 1e-05)
            refs[1][rows] = scale
        else:
            scale = refs[0][rows]
        scale = scale[:, :1]
        gate, up = total[:per] * scale, total[per:] * scale
        made.append(gate / (1.0 + jnp.exp(-gate)) * up)
    out_ref[...] = jnp.concatenate(made, axis=0).astype(BF16)


def hidden_of(keep, width, arrived, scale, features, pair):
    group, both, _ = keep.shape
    rows = group * both // 2
    summed = scale is None
    out = struct((rows, width), BF16)
    return pl.pallas_call(
        functools.partial(hidden_kernel, len(arrived), width, summed, features, pair),
        out_shape=(out, struct((rows, LANES), F32)) if summed else (out,),
        in_specs=[VMEM] * (1 + len(arrived) + (not summed)),
        out_specs=(VMEM,) * (1 + summed),
        name="hidden",
        compiler_params=pltpu.CompilerParams(vmem_limit_bytes=8 * MIB),
        cost_estimate=cost(keep.size * 10, keep.size * 10),
    )(keep, *arrived, *([] if summed else [scale]))


def join_kernel(*refs):
    sources, out_ref = refs[:-1], refs[-1]
    out_ref[...] = jnp.concatenate([ref[...].astype(F32) for ref in sources], axis=0).astype(BF16)


def join(parts):
    rows, width = parts[0].shape
    return pl.pallas_call(
        join_kernel,
        out_shape=struct((rows * len(parts), width), BF16),
        in_specs=[VMEM] * len(parts),
        out_specs=VMEM,
        name="join",
        compiler_params=pltpu.CompilerParams(vmem_limit_bytes=8 * MIB),
        cost_estimate=cost(0, rows * len(parts) * width * 4),
    )(*parts)


def load_down_kernel(first, base_ref, down_hbm, after_ref, held, sems):
    row = pl.multiple_of(base_ref[0] + first, LANES)
    cuts = cuts_of(held.shape[0], 2 * PIECE)
    pairs = [(down_hbm.at[pl.ds(row + a, b - a), :], held.at[pl.ds(a, b - a), :]) for a, b in cuts]
    for copy in start_copies(pairs, sems):
        copy.wait()


def load_down(first, depth, base, weight, after):
    return pl.pallas_call(
        functools.partial(load_down_kernel, first),
        out_shape=struct((depth, weight.shape[1]), BF16),
        in_specs=[SMEM, HBM, VMEM],
        out_specs=VMEM,
        scratch_shapes=[pltpu.SemaphoreType.DMA((len(cuts_of(depth, 2 * PIECE)),))],
        name="load_down",
        compiler_params=pltpu.CompilerParams(vmem_limit_bytes=LOAD_LIMIT * MIB),
        cost_estimate=cost(0, 2 * depth * weight.shape[1]),
    )(base, weight, after)


def down_kernel(first, count, added, fresh, sent, base_ref, *refs):
    refs = list(refs)
    parts, weight, refs = refs[:count], refs[count], refs[count + 1 :]
    before = refs.pop(0) if added else None
    out_ref = refs.pop(0)
    send_ref = refs.pop(0) if sent else None
    if fresh:
        held, sems = refs
        row = pl.multiple_of(base_ref[0] + first, LANES)
        cuts = cuts_of(held.shape[0], 2 * PIECE)
        copies = start_copies([(weight.at[pl.ds(row + a, b - a), :], held.at[pl.ds(a, b - a), :]) for a, b in cuts], sems)
    else:
        held, cuts = weight, [(0, weight.shape[0])]
    hidden = jnp.concatenate([ref[...] for ref in parts], axis=0)
    total = before[...] if added else None
    for i, (a, b) in enumerate(cuts):
        if fresh:
            copies[i].wait()
        term = jnp.dot(hidden[:, a:b], held[a:b, :], preferred_element_type=F32)
        total = term if total is None else total + term
    out_ref[...] = total
    if sent:
        send_ref[...] = squeeze(total)


def down(first, base, parts, weight, before, fresh, sent):
    rows, width = sum(part.shape[0] for part in parts), weight.shape[1]
    depth = parts[0].shape[1]
    added = before is not None
    return pl.pallas_call(
        functools.partial(down_kernel, first, len(parts), added, fresh, sent),
        out_shape=(struct((rows, width), F32),)
        + (struct((rows, width), BF16),) * sent
        + (struct((depth, width), BF16),) * fresh,
        in_specs=[SMEM] + [VMEM] * len(parts) + [HBM if fresh else VMEM] + [VMEM] * added,
        out_specs=(VMEM,) * (1 + sent + fresh),
        scratch_shapes=[pltpu.SemaphoreType.DMA((len(cuts_of(depth, 2 * PIECE)),))] * fresh,
        name="down",
        compiler_params=pltpu.CompilerParams(vmem_limit_bytes=(DOWN_LIMIT if fresh else HELD_LIMIT) * MIB),
        cost_estimate=cost(2 * rows * depth * width, 2 * depth * width),
    )(base, *parts, weight, *([before] if added else []))


def chip_kernel(a_ref, b_ref, state_ref, *outs):
    total = a_ref[...] + expand(b_ref)
    state = state_ref[...] + total
    half = outs[0].shape[1]
    for k in range(2):
        columns = slice(k * half, (k + 1) * half)
        outs[k][...] = state[:, columns]
        outs[2 + k][...] = squeeze(total[:, columns])


def finish_kernel(offsets, per, groups, where_ref, a_ref, b_ref, state_ref, out_ref, *refs):
    sends, (change, state) = refs[: groups - 1], refs[groups - 1 :]
    me, group = where_ref[0], where_ref[1]
    other = expand(b_ref)
    for p, offset in enumerate(offsets):
        first = (me ^ offset) * per
        if per % 8 == 0:
            first = pl.multiple_of(first, 8)
        rows = slice(p * per, (p + 1) * per)
        change[pl.ds(first, per), :] = a_ref[rows, :] + other[rows, :]
        state[pl.ds(first, per), :] = state_ref[rows, :]
    rows = out_ref.shape[0]
    own = pl.ds(pl.multiple_of(group * rows, 8), rows)
    out_ref[...] = state[own, :] + change[own, :]
    for k, ref in enumerate(sends):
        other = pl.multiple_of(lax.rem(group + k + 1, groups) * rows, 8)
        ref[...] = squeeze(change[pl.ds(other, rows), :])


def per_device(counts, tokens, gate_weight, up_weight, down_weight):
    groups, wide, ffn = counts
    stages, gathers = stages_of(wide, SCATTER_BITS), stages_of(wide, GATHER_BITS)
    offsets = [reverse(p, wide.bit_length() - 1) for p in range(wide)]
    rows = tokens.shape[0] * groups
    per = rows // wide
    features = tokens.shape[1] * wide
    share = gate_weight.shape[1] // groups
    edges = [share // LANES * sum(CHUNKS[:k]) // sum(CHUNKS) * LANES for k in range(len(CHUNKS) + 1)]
    chunks = [(a, b - a) for a, b in zip(edges, edges[1:])]
    me, group = lax.axis_index("wide"), lax.axis_index("groups")
    where = jnp.stack([me, group]).astype(jnp.int32)
    base = (group * share).astype(jnp.int32).reshape(1)

    def from_group(value, k):
        return lax.ppermute(value, "groups", [((i + k) % groups, i) for i in range(groups)])

    others = [from_group(tokens, k) for k in range(1, groups)]
    state, x, sumsq = arrange(offsets, per, groups, where, tokens, others)

    def scatter_stage(flips, sends):
        return [swap(send, "wide", flip, wide) for flip, send in zip(flips[1:], sends)]

    gate_weight, up_weight, down_weight = (in_hbm(w) for w in (gate_weight, up_weight, down_weight))
    last = len(chunks) - 1
    gates, downs = {}, {}
    early = load(*chunks[0], base, gate_weight)
    for step in range(STEPS):
        work, previous = [], x
        for c, (first, width) in enumerate(chunks):
            weights, fresh = gates.get(c, (gate_weight, up_weight)), (c not in gates,) * 2
            if fresh[0] and c == 0:
                weights, fresh = (early, up_weight), (False, True)
            size = len(stages[0])
            if step > 0 and c == 0:
                *found, state, x = renew_and_gate_up(per, size, states, halves, weights)
            else:
                found = gate_up(
                    first, width, per, size, base, after(x, previous), sumsq if c == 0 else None, weights, fresh
                )
            previous = found[0]
            if c not in gates:
                gates[c] = tuple(found[size:]) if c else (early, found[size])
            sends = list(found[1:size])
            if TIE and work:
                sends = [after(send, work[-1][1][0]) for send in sends]
            work.append((found[0], scatter_stage(stages[0], sends)))
        for at, flips in enumerate(stages[1:], 1):
            pair = PAIR and at + 1 == len(stages) and len(flips) == 2
            done = []
            for c, (first, width) in enumerate(chunks):
                keep, arrived = work[c]
                if c < last:
                    keep = after(keep, work[c + 1][0])
                elif c - 1 in downs and PRELOAD and step == 0:
                    keep = after(keep, downs[c - 1])
                keep, *sends = add_stage(keep, width, arrived, len(flips), pair)
                done.append((keep, scatter_stage(flips, sends)))
                if PRELOAD and c not in downs:
                    downs[c] = load_down(first, width, base, down_weight, keep)
            work = done
        scale, parts = None, []
        for c, (first, width) in enumerate(chunks):
            keep, arrived = work[c]
            if c < last:
                keep = after(keep, work[c + 1][0])
            elif c in downs:
                keep = after(keep, downs[c])
            made = hidden_of(keep, width, arrived, scale, features, pair)
            scale = made[1] if scale is None else scale
            parts.append([made[0]])
        for flips in reversed(gathers[:-1] if pair else gathers):
            done = []
            for c in range(len(chunks)):
                pieces = parts[c]
                if c < last and len(pieces) > 1:
                    pieces = [after(pieces[0], parts[c + 1][0])] + pieces[1:]
                done.append(pieces[0] if len(pieces) == 1 else join(pieces))
            for c in range(len(chunks)):
                whole = done[c]
                parts[c] = [whole] + [swap(whole, "wide", flip, wide) for flip in flips[1:]]
        change = None
        for c, (first, width) in enumerate(chunks):
            fresh = c not in downs
            if c < last:
                parts[c][0] = after(parts[c][0], parts[c + 1][0])
            found = down(first, base, parts[c], down_weight if fresh else downs[c], change, fresh, c == last)
            change = found[0]
            if fresh:
                downs[c] = found[-1]
        other = swap(found[1], "ffn", 1, ffn)
        if step + 1 < STEPS:
            half = struct((rows, state.shape[1] // 2), F32)
            sent = struct(half.shape, BF16)
            *states, first_send, second_send = pl.pallas_call(
                chip_kernel,
                out_shape=(half, half, sent, sent),
                in_specs=[VMEM] * 3,
                out_specs=(VMEM,) * 4,
                name="chip_sum",
                compiler_params=pltpu.CompilerParams(vmem_limit_bytes=8 * MIB),
                cost_estimate=cost(state.size, state.size * 16),
            )(change, other, state)
            halves = [[from_group(send, k) for k in range(1, groups)] for send in (first_send, second_send)]
    own = struct(tokens.shape, F32)
    out, *sends = pl.pallas_call(
        functools.partial(finish_kernel, offsets, per, groups),
        out_shape=(own,) + (struct(tokens.shape, BF16),) * (groups - 1),
        in_specs=[SMEM] + [VMEM] * 3,
        out_specs=(VMEM,) * groups,
        scratch_shapes=[pltpu.VMEM(state.shape, F32)] * 2,
        name="finish",
        compiler_params=pltpu.CompilerParams(vmem_limit_bytes=8 * MIB),
        cost_estimate=cost(state.size, state.size * 16),
    )(where, change, other, state)
    for k, send in enumerate(sends):
        arrived = from_group(send, groups - 1 - k)
        out = out + expand(arrived)
    return out


def solution(mesh):
    counts = tuple(mesh.shape[axis] for axis in ("groups", "wide", "ffn"))
    return jax.shard_map(
        functools.partial(per_device, counts),
        mesh=mesh,
        in_specs=(P("groups", "wide"), P("wide", "ffn"), P("wide", "ffn"), P("ffn", "wide")),
        out_specs=P("groups", "wide"),
        check_vma=False,
    )
```
